32 devices in a mesh: section: 8 (over y, x, core), expert: 4 (over z).
Axes of the slice: x: 2, y: 2, z: 4, core: 2. Of those that a mesh axis runs over, the one named last changes fastest.
Arguments:
- cotangent: bfloat16 [8, 512, 4096], P('section', 'expert'), may hold values from -6 to 6
- routes: int32 [8, 512, 2], P('section', 'expert'), may hold values from 0 to 3, all different within a row; in each aligned block of 64 rows (0 to 63, 64 to 127, ..., all dimensions but the last counted through in order) at most 64 rows name the same one
- gate_prob: float32 [8, 512, 2], P('section', 'expert'), may hold values from 0.05 to 1
- hidden: bfloat16 [8, 4, 2, 4, 64, 1536], P('section', 'expert'), may hold values from -6 to 6
Outputs:
- grad_pair: bfloat16 [4, 4, 1536, 4096], P(None, 'expert', 'section')
The draws below stay inside these ranges and needn't reach their ends.
Inputs may be any that keep to these rules, and one draw needn't show every extreme that they name: `routes`: each row names 2 different experts. In each aligned block of 64 rows (one micro-batch of one device) no expert is named by more than 64 rows.
All inputs are finite; a program needn't handle non-finite values.
Results may differ from the reference program's by a relative error of at most 0.0059.
Values may be sent and summed in bfloat16 or wider, within the bound.
No kernel may reach another device: no remote copies, remote signals or barrier semaphores. Data moves between devices by JAX's collectives and lax.ppermute only.
A program may use at most 128 MiB of HBM per device.

```python
import math
import jax
import jax.numpy as jnp
import numpy as np
from jax import lax

D = 4096
FF = 1536
TOK_MB = 64
MB = 2
TOP = 2
EXPERTS = 4
CAP = 64
TOKENS = 512
N_SECTION = 8
N_EXPERT = 4


def levels(own_key, dims, cuts, least, top_value):
    gain, own = 1.0, jax.random.fold_in(own_key, 6)
    for dim, parts in cuts:
        heights = jnp.exp(jax.random.uniform(jax.random.fold_in(own, dim), (parts,), jnp.float32, least / len(cuts), top_value / len(cuts)))
        gain = gain * jnp.repeat(heights, dims[dim] // parts).reshape([-1 if axis == dim else 1 for axis in range(len(dims))])
    return gain


def deal_out(key, own, number, rows, count, top, bound, lean):
    sequence = jax.random.permutation(key, count)
    crowded, common = load_shares(count, rows * top, bound, lean, True), load_shares(count, rows * top, bound, lean, False)
    places = jnp.arange(count)

    def named(sizes, turn):
        used = int((sizes > 0).sum())
        fixed = max(1, used // 4)
        passed = fixed + (places - fixed + turn * (used - fixed)) % max(1, count - fixed)
        return jnp.zeros((count,), jnp.int32).at[sequence[jnp.where(places < fixed, places, passed)]].set(jnp.asarray(sizes, jnp.int32))

    sizes = jnp.where(number % 4 == 0, named(crowded, number // 4), named(common, number - number // 4 - 1))
    mixed = jax.random.permutation(jax.random.fold_in(own, 3), count)
    giver, taker = mixed[0:count // 2 * 2:2], mixed[1:count // 2 * 2:2]
    slack = jnp.minimum(sizes[giver] - 1, bound - sizes[taker]) // 2
    slack = jnp.where((giver == sequence[0]) | (taker == sequence[0]) | (sizes[taker] == 0), 0, jnp.maximum(slack, 0))
    passed = jax.random.randint(jax.random.fold_in(own, 4), (count // 2,), 0, 1 << 20) % (slack + 1)
    sizes = sizes.at[giver].add(-passed).at[taker].add(passed)
    members = jnp.searchsorted(jnp.cumsum(sizes), jnp.arange(rows * top), side="right").astype(jnp.int32)
    listing = members.reshape(top, rows).T
    listing = listing[jax.random.permutation(jax.random.fold_in(own, 1), rows)]
    turn = jax.random.randint(jax.random.fold_in(own, 2), (rows, 1), 0, top)
    return jnp.take_along_axis(listing, (jnp.arange(top)[None, :] + turn) % top, axis=1)


def load_shares(amount, total, bound, skew, full):
    portions = [(1 << 20) // math.isqrt(grade ** skew) + 1 for grade in range(1, amount + 1)]
    largest = bound if full else min(bound, max(-(-total // amount), total * portions[0] // sum(portions)))
    least = 1 if total - largest >= amount - 1 else 0
    counts, rest = [largest] + [least] * (amount - 1), total - largest - least * (amount - 1)
    while rest > 0:
        free = [i for i in range(1, amount) if counts[i] < largest] or [i for i in range(1, amount) if counts[i] < bound]
        pool, left = sum([portions[i] for i in free]), rest
        for i in free:
            more = min(bound - counts[i], max(1, left * portions[i] // pool), rest)
            counts[i] = counts[i] + more
            rest = rest - more
    return np.array(counts)


def noise(key, shape, scale, reach, split=(), held_as=jnp.bfloat16):
    drawn = jax.random.normal(key, shape, jnp.float32) * scale
    if len(split) > 0:
        drawn = levels(key, shape, split, -0.22, 0.18) * drawn
    return jnp.clip(drawn, min=-reach, max=reach).astype(held_as)


def setup_inputs(seed: int = 0) -> dict:
    key_list = jax.random.split(jax.random.key(seed), 5)
    cotangent = noise(key_list[0], (N_SECTION, TOKENS, D), 1.0, 6.0, ((0, 8), (1, 4)))
    routes_keys = jax.random.split(jax.random.fold_in(key_list[1], 1), N_SECTION * TOKENS // TOK_MB)
    routes_turns = jax.random.permutation(jax.random.fold_in(key_list[1], 3), N_SECTION * TOKENS // TOK_MB)
    routes = jax.vmap(lambda own, number: deal_out(jax.random.fold_in(key_list[1], 2), own, number, TOK_MB, EXPERTS, TOP, CAP, 2))(routes_keys, routes_turns).reshape((N_SECTION, TOKENS, TOP))
    gate_prob = jnp.clip(jnp.exp(math.log(1.0) - 2.9957323 * jax.random.uniform(key_list[2], (N_SECTION, TOKENS, TOP), jnp.float32) ** levels(key_list[2], (N_SECTION, TOKENS, TOP), ((0, 8), (1, 4)), -0.2, 0.2)), 0.05, 1.0)
    hidden = noise(key_list[3], (N_SECTION, EXPERTS, MB, N_EXPERT, CAP, FF), 1.0, 6.0, ((0, 8), (1, 4)))
    return dict(cotangent=cotangent, routes=routes, gate_prob=gate_prob, hidden=hidden)


def slot_index(route_blk):
    labels = jnp.arange(EXPERTS, dtype=jnp.int32)
    hits = (route_blk[:, :, None] == labels).astype(jnp.int32)
    per_token = lax.optimization_barrier(jnp.sum(hits, axis=1))
    before = jnp.cumsum(per_token, axis=0) - per_token
    return lax.optimization_barrier(jnp.sum(hits * before[:, None, :], axis=2))

def pack_block(cot_blk, route_blk, prob_blk):
    slots = slot_index(route_blk)
    flat = (route_blk * CAP + slots).reshape(-1).astype(jnp.int32)
    weighted = (prob_blk[:, :, None] * cot_blk[:, None, :].astype(jnp.float32)).astype(jnp.bfloat16)
    empty = jnp.zeros((EXPERTS * CAP, D), jnp.bfloat16)
    return empty.at[flat].set(weighted.reshape(-1, D)).reshape(EXPERTS, CAP, D)

def section_grad(cot, route, prob, hid):
    blocks = N_EXPERT * MB
    packed = jax.vmap(pack_block)(cot.reshape(blocks, TOK_MB, D), route.reshape(blocks, TOK_MB, TOP), prob.reshape(blocks, TOK_MB, TOP))
    packed = packed.reshape(N_EXPERT, MB, EXPERTS, CAP, D).transpose(2, 1, 0, 3, 4)

    def one_expert(pair):
        acts, rows = pair
        total = lax.dot_general(acts.reshape(-1, FF), rows.reshape(-1, D), (((0,), (0,)), ((), ())), preferred_element_type=jnp.float32)
        return total.astype(jnp.bfloat16)
    return lax.map(one_expert, (hid, packed))

def reference(cotangent, routes, gate_prob, hidden):

    def pair_sum(index):
        mirror = N_SECTION - 1 - index
        lower = section_grad(cotangent[index], routes[index], gate_prob[index], hidden[index])
        upper = section_grad(cotangent[mirror], routes[mirror], gate_prob[mirror], hidden[mirror])
        return (lower.astype(jnp.float32) + upper.astype(jnp.float32)).astype(jnp.bfloat16)
    return lax.map(pair_sum, jnp.arange(N_SECTION // 2, dtype=jnp.int32))
```

```python
from functools import partial

import jax
import jax.numpy as jnp
from jax import lax
from jax.experimental import pallas as pl
from jax.experimental.pallas import tpu as pltpu
from jax.sharding import PartitionSpec as P

VMEM = 56 * 1024 * 1024


def token_acts_kernel(expert_ref, meta_ref, hid_ref, out_ref, *, top, capacity, tok_block):
    tokens = meta_ref.shape[-1]
    slots = hid_ref.shape[1] * hid_ref.shape[3]
    ff_width = hid_ref.shape[-1]
    expert = expert_ref[0].astype(jnp.float32)
    hit = jnp.zeros((1, tokens), jnp.float32)
    gate = jnp.zeros((1, tokens), jnp.float32)
    for k in range(top):
        named = (meta_ref[0, 0, k : k + 1, :] == expert).astype(jnp.float32)
        hit = hit + named
        gate = gate + named * meta_ref[0, 0, top + k : top + k + 1, :]
    row = lax.broadcasted_iota(jnp.int32, (tokens, tokens), 0)
    col = lax.broadcasted_iota(jnp.int32, (tokens, tokens), 1)
    earlier = ((row // tok_block == col // tok_block) & (row < col)).astype(jnp.float32)
    before = jnp.dot(jnp.broadcast_to(hit, (8, tokens)), earlier, preferred_element_type=jnp.float32)[:1]
    block = lax.broadcasted_iota(jnp.int32, (1, tokens), 1) // tok_block
    place = jnp.where(hit > 0, block * capacity + before.astype(jnp.int32), -1)
    pick = (lax.broadcasted_iota(jnp.int32, (slots, tokens), 0) == place).astype(jnp.bfloat16)
    hid = hid_ref[0, :, 0].reshape(slots, ff_width)
    rows = lax.dot_general(hid, pick, (((0,), (0,)), ((), ())), preferred_element_type=jnp.float32)
    out_ref[0] = (rows * gate).astype(jnp.bfloat16).reshape(out_ref.shape[1:])


def token_acts(meta, hidden, sections, tok_block):
    replicas, sources, fields, tokens = meta.shape
    mb_count, _, capacity, ff_width = hidden.shape[1:]
    rows = ff_width // sections
    expert = lax.axis_index("expert").astype(jnp.int32).reshape(1)
    return pl.pallas_call(
        partial(token_acts_kernel, top=fields // 2, capacity=capacity, tok_block=tok_block),
        grid_spec=pltpu.PrefetchScalarGridSpec(
            num_scalar_prefetch=1,
            grid=(replicas, sources),
            in_specs=[
                pl.BlockSpec((1, 1, fields, tokens), lambda r, j, e: (r, j, 0, 0)),
                pl.BlockSpec((1, mb_count, 1, capacity, ff_width), lambda r, j, e: (r, 0, j, 0, 0)),
            ],
            out_specs=pl.BlockSpec((1, sections, rows, tokens), lambda r, j, e: (r, 0, 0, j)),
        ),
        out_shape=jax.ShapeDtypeStruct((replicas, sections, rows, sources * tokens), jnp.bfloat16),
        compiler_params=pltpu.CompilerParams(vmem_limit_bytes=VMEM),
    )(expert, meta, hidden)


def product_kernel(*refs):
    acts, cots, out_ref, packed = refs[:2], refs[2:-2], refs[-2], refs[-1]
    tokens = cots[0].shape[0]
    for i, cot in enumerate(cots):
        packed[i * tokens : (i + 1) * tokens] = cot[...]
    half = packed.shape[0] // 2

    @pl.loop(0, out_ref.shape[0])
    def _(r):
        total = jnp.dot(acts[0][0, r], packed[:half], preferred_element_type=jnp.float32)
        total += jnp.dot(acts[1][0, r], packed[half:], preferred_element_type=jnp.float32)
        out_ref[r] = total.astype(jnp.bfloat16)


def product(own_acts, mirror_acts, cots, tile):
    _, sections, rows, depth = own_acts.shape
    tokens, width = cots[0].shape
    acts_spec = pl.BlockSpec((1, sections, rows, depth), lambda n: (0, 0, 0, 0))
    cot_spec = pl.BlockSpec((tokens, tile), lambda n: (0, n))
    return pl.pallas_call(
        product_kernel,
        grid=(width // tile,),
        in_specs=[acts_spec, acts_spec] + [cot_spec] * len(cots),
        out_specs=pl.BlockSpec((sections, rows, tile), lambda n: (0, 0, n)),
        out_shape=jax.ShapeDtypeStruct((sections, rows, width), jnp.bfloat16),
        scratch_shapes=[pltpu.VMEM((len(cots) * tokens, tile), jnp.bfloat16)],
        compiler_params=pltpu.CompilerParams(vmem_limit_bytes=VMEM),
        cost_estimate=pl.CostEstimate(
            flops=4 * sections * rows * depth * width,
            bytes_accessed=4 * (sections * rows * depth + depth * width) + 2 * sections * rows * width,
            transcendentals=0,
        ),
    )(own_acts, mirror_acts, *cots)


def join_kernel(*refs):
    pieces, out_ref = refs[:-1], refs[-1]
    width = pieces[0].shape[-1]
    for i, piece in enumerate(pieces):
        out_ref[0, 0, :, i * width : (i + 1) * width] = piece[0]


def join(chunks):
    sections, rows, width = chunks[0].shape
    half, count = sections // 2, len(chunks)
    lower = pl.BlockSpec((1, rows, width), lambda p: (p, 0, 0))
    upper = pl.BlockSpec((1, rows, width), lambda p: (sections - 1 - p, 0, 0))
    return pl.pallas_call(
        join_kernel,
        grid=(half,),
        in_specs=[lower] * count + [upper] * count,
        out_specs=pl.BlockSpec((1, 1, rows, 2 * count * width), lambda p: (p, 0, 0, 0)),
        out_shape=jax.ShapeDtypeStruct((half, 1, rows, 2 * count * width), jnp.bfloat16),
        compiler_params=pltpu.CompilerParams(vmem_limit_bytes=VMEM),
    )(*chunks, *chunks)


def local(cotangent, routes, gate_prob, hidden):
    n_section = lax.axis_size("section")
    n_expert = lax.axis_size("expert")
    section = lax.axis_index("section")
    expert = lax.axis_index("expert")
    mb_count = hidden.shape[2]
    tokens, width = cotangent.shape[1:]
    half_width = width // 2
    chunks = 2
    chunk_width = half_width // chunks
    mirror = [(i, n_section - 1 - i) for i in range(n_section)]
    upper = section >= n_section // 2

    cot = cotangent[0]
    low, high = cot[:, :half_width], cot[:, half_width:]
    kept = jnp.where(upper, high, low)
    given = jnp.where(upper, low, high)
    meta = jnp.concatenate([routes[0].T.astype(jnp.float32), gate_prob[0].T], 0)
    metas = lax.all_gather(meta, "expert")
    mirror_metas = lax.ppermute(metas, "section", mirror)
    taken = [
        lax.ppermute(given[:, c * chunk_width : (c + 1) * chunk_width], "section", mirror) for c in range(chunks)
    ]
    own = hidden[0, 0][None]
    mirrored = lax.ppermute(own, "section", mirror)
    own_acts = token_acts(metas[None], own, n_section, tokens // mb_count)
    mirror_acts = token_acts(mirror_metas[None], mirrored, n_section, tokens // mb_count)

    landed = []
    for c in range(chunks):
        mine = kept[:, c * chunk_width : (c + 1) * chunk_width]
        cots = []
        for block in (mine, taken[c]):
            whole = lax.all_gather(block, "expert", tiled=True)
            cots.append(whole)
        sums = product(own_acts, mirror_acts, cots, chunk_width // 4)
        landed.append(lax.all_to_all(sums, "section", split_axis=0, concat_axis=0, tiled=True))
    return join(landed)


def solution(mesh):
    return jax.shard_map(
        local,
        mesh=mesh,
        in_specs=(
            P("section", "expert", None),
            P("section", "expert", None),
            P("section", "expert", None),
            P("section", "expert", None, None, None),
        ),
        out_specs=P(None, "expert", "section", None),
        check_vma=False,
    )
```

```python
from functools import partial

import jax
import jax.numpy as jnp
from jax import lax
from jax.experimental import pallas as pl
from jax.experimental.pallas import tpu as pltpu
from jax.sharding import PartitionSpec as P

VMEM = 56 * 1024 * 1024


def token_acts_kernel(sources_ref, ids_ref, meta_ref, hid_ref, *refs, groups, top, capacity, tok_block):
    outs, rows_ref = refs[:-1], refs[-1]
    count = hid_ref.shape[1]
    tokens = rows_ref.shape[-1] // count
    slots = hid_ref.shape[0] * hid_ref.shape[2]
    expert = ids_ref[0].astype(jnp.float32)

    def field(i):
        return meta_ref[:, i * tokens : (i + 1) * tokens]

    hit = jnp.zeros((count, tokens), jnp.float32)
    gate = jnp.zeros((count, tokens), jnp.float32)
    for k in range(top):
        named = (field(k) == expert).astype(jnp.float32)
        hit = hit + named
        gate = gate + named * field(top + k)
    row = lax.broadcasted_iota(jnp.int32, (tokens, tokens), 0)
    col = lax.broadcasted_iota(jnp.int32, (tokens, tokens), 1)
    earlier = ((row // tok_block == col // tok_block) & (row < col)).astype(jnp.float32)
    before = jnp.dot(hit, earlier, preferred_element_type=jnp.float32)
    block = lax.broadcasted_iota(jnp.int32, (count, tokens), 1) // tok_block
    place = jnp.where(hit > 0, block * capacity + before.astype(jnp.int32), -1)
    slot = lax.broadcasted_iota(jnp.int32, (slots, tokens), 0)
    for i in range(count):
        source = sources_ref[i]
        pick = (slot == place[i : i + 1]).astype(jnp.bfloat16)
        hid = hid_ref[:, source].reshape(slots, hid_ref.shape[-1])
        rows = lax.dot_general(hid, pick, (((0,), (0,)), ((), ())), preferred_element_type=jnp.float32)
        rows = (rows * gate[i : i + 1]).astype(jnp.bfloat16)
        at = pl.ds(pl.multiple_of(source * tokens, tokens), tokens)
        rows_ref[:, :, at] = rows.reshape(rows_ref.shape[0], rows_ref.shape[1], tokens)
    for masks, out in zip(groups, outs):
        for i, mask in enumerate(masks):
            out[i] = rows_ref[ids_ref[1] ^ mask]


def token_acts(sources, metas, hidden, groups, top, tok_block, tokens):
    sections = lax.axis_size("section")
    mb_count, count, capacity, ff_width = hidden.shape
    rows = ff_width // sections
    depth = count * tokens
    ids = jnp.stack([lax.axis_index("expert"), lax.axis_index("section")]).astype(jnp.int32)
    return pl.pallas_call(
        partial(token_acts_kernel, groups=groups, top=top, capacity=capacity, tok_block=tok_block),
        grid_spec=pltpu.PrefetchScalarGridSpec(
            num_scalar_prefetch=2,
            grid=(),
            in_specs=[pl.BlockSpec(memory_space=pltpu.VMEM)] * 2,
            out_specs=[pl.BlockSpec(memory_space=pltpu.VMEM)] * len(groups),
            scratch_shapes=[pltpu.VMEM((sections, rows, depth), jnp.bfloat16)],
        ),
        out_shape=[jax.ShapeDtypeStruct((len(masks), rows, depth), jnp.bfloat16) for masks in groups],
        compiler_params=pltpu.CompilerParams(vmem_limit_bytes=VMEM),
        cost_estimate=pl.CostEstimate(
            flops=2 * mb_count * capacity * ff_width * depth,
            bytes_accessed=2 * ff_width * count * (mb_count * capacity + tokens),
            transcendentals=0,
        ),
    )(sources, ids, metas, hidden)


def product_kernel(places_ref, own_ref, mirror_ref, *refs, tokens, terms):
    count, rows, depth = own_ref.shape
    cots, outs, packed = refs[: -1 - count], refs[-1 - count : -1], refs[-1]
    at = 0
    for group in terms:
        for i in range(cots[group[0]].shape[0]):
            block = cots[group[0]][i]
            for other in group[1:]:
                block = block + cots[other][i]
            place = places_ref[at] * tokens
            for part in range(block.shape[0] // tokens):
                start = pl.multiple_of(place + part * depth, tokens)
                packed[pl.ds(start, tokens)] = block[part * tokens : (part + 1) * tokens]
            at += 1
    own = jnp.dot(own_ref[...].reshape(count * rows, depth), packed[:depth], preferred_element_type=jnp.float32)
    mirror = jnp.dot(mirror_ref[...].reshape(count * rows, depth), packed[depth:], preferred_element_type=jnp.float32)
    for i, out in enumerate(outs):
        j = count - 1 - i
        total = own[i * rows : (i + 1) * rows] + mirror[j * rows : (j + 1) * rows]
        out[...] = total.astype(jnp.bfloat16)


def product(places, own_acts, mirror_acts, cots, tokens, tile):
    count, rows, depth = own_acts.shape
    arrays = [array for entry in cots for array in entry]
    terms, at = [], 0
    for entry in cots:
        terms.append(list(range(at, at + len(entry))))
        at += len(entry)
    width = arrays[0].shape[-1]
    acts_spec = pl.BlockSpec((count, rows, depth), lambda n, src: (0, 0, 0))
    cot_specs = [pl.BlockSpec((*array.shape[:2], tile), lambda n, src: (0, 0, n)) for array in arrays]
    return pl.pallas_call(
        partial(product_kernel, tokens=tokens, terms=terms),
        grid_spec=pltpu.PrefetchScalarGridSpec(
            num_scalar_prefetch=1,
            grid=(width // tile,),
            in_specs=[acts_spec, acts_spec] + cot_specs,
            out_specs=[pl.BlockSpec((rows, tile), lambda n, src: (0, n))] * count,
            scratch_shapes=[pltpu.VMEM((2 * depth, tile), jnp.bfloat16)],
        ),
        out_shape=[jax.ShapeDtypeStruct((rows, width), jnp.bfloat16)] * count,
        compiler_params=pltpu.CompilerParams(vmem_limit_bytes=VMEM),
        cost_estimate=pl.CostEstimate(
            flops=4 * count * rows * depth * width,
            bytes_accessed=4 * (count * rows * depth + depth * width) + 2 * count * rows * width,
            transcendentals=0,
        ),
    )(places, own_acts, mirror_acts, *arrays)


def join_kernel(*refs, sections, offset):
    pieces = refs[:sections]
    out, sem = refs[-2:]
    section = lax.axis_index("section")
    width = pieces[0].shape[-1]
    copies = []
    for mask, piece in enumerate(pieces):
        source = section ^ mask
        upper = (source >= sections // 2).astype(jnp.int32)
        pair = source + upper * (sections - 1 - 2 * source)
        column = pl.multiple_of(upper * (out.shape[-1] // 2) + offset, 128)
        copies.append(pltpu.make_async_copy(piece, out.at[pair, 0, :, pl.ds(column, width)], sem.at[mask]))
    for copy in copies:
        copy.start()
    for copy in copies:
        copy.wait()


def join(pieces, offset, half_width, out=None):
    sections = len(pieces)
    rows = pieces[0].shape[0]
    shape = jax.ShapeDtypeStruct((sections // 2, 1, rows, 2 * half_width), jnp.bfloat16)
    first = out is None
    operands = tuple(pieces) if first else (*pieces, out)
    return pl.pallas_call(
        partial(join_kernel, sections=sections, offset=offset),
        in_specs=[pl.BlockSpec(memory_space=pltpu.VMEM)] * sections + [pl.BlockSpec(memory_space=pl.ANY)] * (not first),
        out_specs=pl.BlockSpec(memory_space=pl.ANY),
        out_shape=shape,
        scratch_shapes=[pltpu.SemaphoreType.DMA((sections,))],
        input_output_aliases={} if first else {sections: 0},
        compiler_params=pltpu.CompilerParams(vmem_limit_bytes=VMEM),
    )(*operands)


def shift(block, axis, size, step):
    return lax.ppermute(block, axis, [(i, (i + step) % size) for i in range(size)])


def ring(block, axis, size):
    return [block] + [shift(block, axis, size, step) for step in range(1, size)]


def local(cotangent, routes, gate_prob, hidden):
    n_section = lax.axis_size("section")
    n_expert = lax.axis_size("expert")
    section = lax.axis_index("section")
    expert = lax.axis_index("expert")
    mb_count = hidden.shape[2]
    tokens, width = cotangent.shape[1:]
    top = routes.shape[2]
    half_width = width // 2
    widths = [half_width * 5 // 8, half_width * 3 // 8]
    offsets = [sum(widths[:c]) for c in range(len(widths))]
    mirror = [(i, n_section - 1 - i) for i in range(n_section)]
    upper = section >= n_section // 2
    quarter = n_section // 4
    near = list(range(quarter, n_section - quarter))
    groups = [near, [mask for mask in range(n_section) if mask not in near]]
    steps = jnp.arange(n_expert, dtype=jnp.int32)
    behind = lax.rem(expert - steps + n_expert, n_expert).astype(jnp.int32)
    short = n_expert == 4
    meta = jnp.concatenate([routes[0].astype(jnp.float32), gate_prob[0]], 1).T.reshape(-1)
    metas = jnp.stack(ring(meta, "expert", n_expert)) if short else lax.all_gather(meta, "expert")
    order = behind if short else steps
    acts = token_acts(order, metas, hidden[0, 0], groups, top, tokens // mb_count, tokens)
    cot = cotangent[0]
    kept, given = [], []
    for offset, span in zip(offsets, widths):
        low = cot[:, offset : offset + span]
        high = cot[:, half_width + offset : half_width + offset + span]
        kept.append(jnp.where(upper, high, low))
        given.append(jnp.where(upper, low, high))
    taken = [lax.ppermute(given[0], "section", mirror)]
    if short:
        kept_first, kept_back = shift(kept[0], "expert", n_expert, 1), shift(kept[0], "expert", n_expert, 3)
        *held, taken[0] = lax.optimization_barrier((*acts, taken[0]))
        mirror_acts = [lax.ppermute(group, "section", mirror) for group in held]
        taken.append(lax.ppermute(given[1], "section", mirror))
        kept_first, taken[0] = lax.optimization_barrier((kept_first, taken[0]))
        taken_first, taken_back = shift(taken[0], "expert", n_expert, 1), shift(taken[0], "expert", n_expert, 3)
        both = jnp.concatenate([kept[0], taken[0]])
        both, taken_first, taken_back, mirror_acts[0], taken[1] = lax.optimization_barrier(
            (both, taken_first, taken_back, mirror_acts[0], taken[1])
        )
        across = lax.ppermute(both, "expert", [(0, 2), (3, 1)])
        first = jnp.concatenate([kept_first, taken_first])
        back = jnp.concatenate([kept_back, taken_back])
        passed = lax.ppermute(jnp.where(expert == 2, first, back), "expert", [(2, 3), (1, 0)])
        across, passed, mirror_acts[1] = lax.optimization_barrier((across, passed, mirror_acts[1]))
        cots = [[(both[None],), (first[None],), (across[None], passed[None]), (back[None],)]]
        orders = [behind, steps]
        later = jnp.broadcast_to(jnp.concatenate([kept[1], taken[1]]), (n_expert, 2 * tokens, widths[1]))
    else:
        taken.append(lax.ppermute(given[1], "section", mirror))
        mirror_acts = [lax.ppermute(group, "section", mirror) for group in acts]
        cots = [[(lax.all_gather(jnp.concatenate([a, b]), "expert"),)] for a, b in zip(kept, taken)]
        orders = [steps] * len(cots)

    out = None
    for c, (offset, span) in enumerate(zip(offsets, widths)):
        pieces = [None] * n_section
        for g, masks in enumerate(groups):
            sums = product(orders[c], acts[g], mirror_acts[g], cots[c], tokens, span // 2)
            if short and c == 0 and g == 0:
                later, cots[0] = lax.optimization_barrier((later, cots[0]))
                cots.append([(lax.all_to_all(later, "expert", split_axis=0, concat_axis=0, tiled=True),)])
            for mask, rows in zip(masks, sums):
                pieces[mask] = rows
                if mask:
                    pieces[mask] = lax.ppermute(rows, "section", [(i, i ^ mask) for i in range(n_section)])
        if c == 0:
            sent = [1, 2, n_section - 2, n_section - 1]
            early, cots[1] = lax.optimization_barrier(([pieces[mask] for mask in sent], cots[1]))
            for mask, rows in zip(sent, early):
                pieces[mask] = rows
        out = join(pieces, offset, half_width, out)
    return out


def solution(mesh):
    return jax.shard_map(
        local,
        mesh=mesh,
        in_specs=(
            P("section", "expert", None),
            P("section", "expert", None),
            P("section", "expert", None),
            P("section", "expert", None, None, None),
        ),
        out_specs=P(None, "expert", "section", None),
        check_vma=False,
    )
```

```python
from functools import partial

import jax
import jax.numpy as jnp
from jax import lax
from jax.experimental import pallas as pl
from jax.experimental.pallas import tpu as pltpu
from jax.sharding import PartitionSpec as P

VMEM = 60 * 1024 * 1024
LONG = pl.CostEstimate(flops=10**11, bytes_accessed=10**6, transcendentals=0)
SHORT = pl.CostEstimate(flops=10**6, bytes_accessed=10**3, transcendentals=0)


def token_acts_kernel(meta_ref, hid_ref, *refs, groups, top, capacity, tok_block, in_ring):
    outs, rows_ref = refs[:-1], refs[-1]
    count = hid_ref.shape[1]
    tokens = rows_ref.shape[-1] // count
    slots = hid_ref.shape[0] * hid_ref.shape[2]
    me, section = lax.axis_index("expert"), lax.axis_index("section")
    expert = me.astype(jnp.float32)

    def field(i):
        return meta_ref[:, i * tokens : (i + 1) * tokens]

    hit = jnp.zeros((count, tokens), jnp.float32)
    gate = jnp.zeros((count, tokens), jnp.float32)
    for k in range(top):
        named = (field(k) == expert).astype(jnp.float32)
        hit = hit + named
        gate = gate + named * field(top + k)
    row = lax.broadcasted_iota(jnp.int32, (tokens, tokens), 0)
    col = lax.broadcasted_iota(jnp.int32, (tokens, tokens), 1)
    earlier = ((row // tok_block == col // tok_block) & (row < col)).astype(jnp.float32)
    before = jnp.dot(hit, earlier, preferred_element_type=jnp.float32)
    block = lax.broadcasted_iota(jnp.int32, (count, tokens), 1) // tok_block
    place = jnp.where(hit > 0, block * capacity + before.astype(jnp.int32), -1)
    slot = lax.broadcasted_iota(jnp.int32, (slots, tokens), 0)
    for i in range(count):
        source = lax.rem(me + (count - i), count) if in_ring else i
        pick = (slot == place[i : i + 1]).astype(jnp.bfloat16)
        hid = hid_ref[:, source].reshape(slots, hid_ref.shape[-1])
        rows = lax.dot_general(hid, pick, (((0,), (0,)), ((), ())), preferred_element_type=jnp.float32)
        rows = (rows * gate[i : i + 1]).astype(jnp.bfloat16)
        at = pl.ds(pl.multiple_of(source * tokens, tokens), tokens)
        rows_ref[:, :, at] = rows.reshape(rows_ref.shape[0], rows_ref.shape[1], tokens)
    for masks, out in zip(groups, outs):
        for i, mask in enumerate(masks):
            out[i] = rows_ref[section ^ mask]


def token_acts(metas, hidden, groups, top, tok_block, in_ring):
    sections = lax.axis_size("section")
    mb_count, count, capacity, ff_width = hidden.shape
    rows = ff_width // sections
    depth = count * metas.shape[1] // (2 * top)
    return pl.pallas_call(
        partial(token_acts_kernel, groups=groups, top=top, capacity=capacity, tok_block=tok_block, in_ring=in_ring),
        in_specs=[pl.BlockSpec(memory_space=pltpu.VMEM)] * 2,
        out_specs=[pl.BlockSpec(memory_space=pltpu.VMEM)] * len(groups),
        out_shape=[jax.ShapeDtypeStruct((len(masks), rows, depth), jnp.bfloat16) for masks in groups],
        scratch_shapes=[pltpu.VMEM((sections, rows, depth), jnp.bfloat16)],
        compiler_params=pltpu.CompilerParams(vmem_limit_bytes=VMEM),
        cost_estimate=LONG,
    )(metas, hidden)


def product_kernel(own_ref, mirror_ref, *refs, tokens, layout):
    count, rows, depth = own_ref.shape
    cots, outs, packed = refs[: -1 - count], refs[-1 - count : -1], refs[-1]
    sources = depth // tokens
    me = lax.axis_index("expert")
    for cot, (behind, replica) in zip(cots, layout):
        for i in range(cot.shape[0]):
            source = i if behind is None else lax.rem(me + (sources - behind), sources)
            for part in range(cot.shape[1] // tokens):
                start = pl.multiple_of(source * tokens + (replica + part) * depth, tokens)
                packed[pl.ds(start, tokens)] = cot[i, part * tokens : (part + 1) * tokens]
    own = jnp.dot(own_ref[...].reshape(count * rows, depth), packed[:depth], preferred_element_type=jnp.float32)
    mirror = jnp.dot(mirror_ref[...].reshape(count * rows, depth), packed[depth:], preferred_element_type=jnp.float32)
    for i, out in enumerate(outs):
        j = count - 1 - i
        total = own[i * rows : (i + 1) * rows] + mirror[j * rows : (j + 1) * rows]
        out[...] = total.astype(jnp.bfloat16)


def product(own_acts, mirror_acts, cots, layout, tokens, tile):
    count, rows, depth = own_acts.shape
    width = cots[0].shape[-1]
    acts_spec = pl.BlockSpec((count, rows, depth), lambda n: (0, 0, 0))
    return pl.pallas_call(
        partial(product_kernel, tokens=tokens, layout=layout),
        grid=(width // tile,),
        in_specs=[acts_spec, acts_spec] + [pl.BlockSpec((*cot.shape[:2], tile), lambda n: (0, 0, n)) for cot in cots],
        out_specs=[pl.BlockSpec((rows, tile), lambda n: (0, n))] * count,
        out_shape=[jax.ShapeDtypeStruct((rows, width), jnp.bfloat16)] * count,
        scratch_shapes=[pltpu.VMEM((2 * depth, tile), jnp.bfloat16)],
        compiler_params=pltpu.CompilerParams(vmem_limit_bytes=VMEM),
        cost_estimate=SHORT,
    )(own_acts, mirror_acts, *cots)


def join_kernel(*refs, sections, offset):
    pieces = refs[:sections]
    out, sem = refs[-2:]
    section = lax.axis_index("section")
    width = pieces[0].shape[-1]
    copies = []
    for mask, piece in enumerate(pieces):
        source = section ^ mask
        upper = (source >= sections // 2).astype(jnp.int32)
        pair = source + upper * (sections - 1 - 2 * source)
        column = pl.multiple_of(upper * (out.shape[-1] // 2) + offset, 128)
        copies.append(pltpu.make_async_copy(piece, out.at[pair, 0, :, pl.ds(column, width)], sem.at[mask]))
    for copy in copies:
        copy.start()
    for copy in copies:
        copy.wait()


def join(pieces, offset, half_width, out=None):
    sections = len(pieces)
    rows = pieces[0].shape[0]
    shape = jax.ShapeDtypeStruct((sections // 2, 1, rows, 2 * half_width), jnp.bfloat16)
    first = out is None
    operands = tuple(pieces) if first else (*pieces, out)
    return pl.pallas_call(
        partial(join_kernel, sections=sections, offset=offset),
        in_specs=[pl.BlockSpec(memory_space=pltpu.VMEM)] * sections + [pl.BlockSpec(memory_space=pl.ANY)] * (not first),
        out_specs=pl.BlockSpec(memory_space=pl.ANY),
        out_shape=shape,
        scratch_shapes=[pltpu.SemaphoreType.DMA((sections,))],
        input_output_aliases={} if first else {sections: 0},
        compiler_params=pltpu.CompilerParams(vmem_limit_bytes=VMEM),
    )(*operands)


def shift(block, axis, size, step):
    return lax.ppermute(block, axis, [(i, (i + step) % size) for i in range(size)])


def ring(block, axis, size):
    return [block] + [shift(block, axis, size, step) for step in range(1, size)]


def repeat_kernel(*refs):
    blocks, out = refs[:-2], refs[-1]
    at = 0
    for block in blocks:
        out[0, at : at + block.shape[0]] = block[...]
        at += block.shape[0]


def repeat(blocks, after, count):
    rows, width = sum(block.shape[0] for block in blocks), blocks[0].shape[1]
    return pl.pallas_call(
        repeat_kernel,
        grid=(count,),
        in_specs=[pl.BlockSpec(block.shape, lambda i: (0, 0)) for block in blocks] + [pl.BlockSpec(memory_space=pl.ANY)],
        out_specs=pl.BlockSpec((1, rows, width), lambda i: (i, 0, 0)),
        out_shape=jax.ShapeDtypeStruct((count, rows, width), blocks[0].dtype),
        compiler_params=pltpu.CompilerParams(vmem_limit_bytes=VMEM),
        cost_estimate=LONG,
    )(*blocks, after)


def local(cotangent, routes, gate_prob, hidden):
    n_section = lax.axis_size("section")
    n_expert = lax.axis_size("expert")
    section = lax.axis_index("section")
    expert = lax.axis_index("expert")
    mb_count = hidden.shape[2]
    tokens, width = cotangent.shape[1:]
    top = routes.shape[2]
    half_width = width // 2
    widths = [half_width * 9 // 16, half_width * 7 // 16]
    offsets = [sum(widths[:c]) for c in range(len(widths))]
    mirror = [(i, n_section - 1 - i) for i in range(n_section)]
    upper = section >= n_section // 2
    quarter = n_section // 4
    near = [start + i for i in range(quarter // 2) for start in (quarter, 2 * quarter)]
    near += [n_section - 1 - mask for mask in reversed(near)]
    groups = [[mask for mask in range(n_section) if mask not in near], near]
    short = n_expert == 4
    meta = jnp.concatenate([routes[0].astype(jnp.float32), gate_prob[0]], 1).T.reshape(-1)
    metas = jnp.stack(ring(meta, "expert", n_expert)) if short else lax.all_gather(meta, "expert")
    acts = token_acts(metas, hidden[0, 0], groups, top, tokens // mb_count, short)
    cot = cotangent[0]
    kept, given = [], []
    for offset, span in zip(offsets, widths):
        low = cot[:, offset : offset + span]
        high = cot[:, half_width + offset : half_width + offset + span]
        kept.append(jnp.where(upper, high, low))
        given.append(jnp.where(upper, low, high))
    taken = [lax.ppermute(block, "section", mirror) for block in given]
    if short:
        kept_first = shift(kept[0], "expert", n_expert, 1)
        *held, taken[0], kept_first = lax.optimization_barrier((*acts, taken[0], kept_first))
        mirror_acts = [lax.ppermute(group, "section", mirror) for group in held]
        both = jnp.concatenate([kept[0], taken[0]])
        taken_first = shift(taken[0], "expert", n_expert, 1)
        back = shift(both, "expert", n_expert, 3)
        both, taken_first, back, mirror_acts[0], taken[1] = lax.optimization_barrier(
            (both, taken_first, back, mirror_acts[0], taken[1])
        )
        chosen = jnp.where(expert == 2, jnp.concatenate([kept_first, taken_first]), jnp.where(expert == 1, back, both))
        passed = lax.ppermute(chosen, "expert", [(0, 2), (2, 3), (3, 1), (1, 0)])
        passed, mirror_acts[1] = lax.optimization_barrier((passed, mirror_acts[1]))
        later = repeat([kept[1], taken[1]], chosen, n_expert)
        later, passed = lax.optimization_barrier((later, passed))
        later = lax.all_to_all(later, "expert", split_axis=0, concat_axis=0, tiled=True)
        cots = [[block[None] for block in (both, kept_first, taken_first, passed, back)], [later]]
        layouts = [[(0, 0), (1, 0), (1, 1), (2, 0), (3, 0)], [(None, 0)]]
    else:
        mirror_acts = [lax.ppermute(group, "section", mirror) for group in acts]
        cots = [[lax.all_gather(jnp.concatenate([a, b]), "expert")] for a, b in zip(kept, taken)]
        layouts = [[(None, 0)]] * len(cots)

    out = None
    for c, (offset, span) in enumerate(zip(offsets, widths)):
        pieces = [None] * n_section
        for g, masks in enumerate(groups):
            sums = list(product(acts[g], mirror_acts[g], cots[c], layouts[c], tokens, span // 3 if span % 384 == 0 else span))
            for mask, rows in zip(masks, sums):
                pieces[mask] = rows
                if mask:
                    pieces[mask] = lax.ppermute(rows, "section", [(i, i ^ mask) for i in range(n_section)])
        if c == 0:
            sent = [1, near[0], near[1], n_section - 2, n_section - 1]
            early, cots[c + 1] = lax.optimization_barrier(([pieces[mask] for mask in sent], cots[c + 1]))
            for mask, rows in zip(sent, early):
                pieces[mask] = rows
        out = join(pieces, offset, half_width, out)
    return out


def solution(mesh):
    return jax.shard_map(
        local,
        mesh=mesh,
        in_specs=(
            P("section", "expert", None),
            P("section", "expert", None),
            P("section", "expert", None),
            P("section", "expert", None, None, None),
        ),
        out_specs=P(None, "expert", "section", None),
        check_vma=False,
    )
```

```python
from functools import partial

import jax
import jax.numpy as jnp
from jax import lax
from jax.experimental import pallas as pl
from jax.experimental.pallas import tpu as pltpu
from jax.sharding import PartitionSpec as P

VMEM = 60 * 1024 * 1024
LONG = pl.CostEstimate(flops=10**11, bytes_accessed=10**6, transcendentals=0)
SHORT = pl.CostEstimate(flops=10**6, bytes_accessed=10**3, transcendentals=0)


def token_acts_kernel(meta_ref, hid_ref, *refs, groups, top, capacity, tok_block, in_ring):
    outs, rows_ref = refs[:-1], refs[-1]
    count = hid_ref.shape[1]
    tokens = rows_ref.shape[-1] // count
    slots = hid_ref.shape[0] * hid_ref.shape[2]
    me, section = lax.axis_index("expert"), lax.axis_index("section")
    expert = me.astype(jnp.float32)

    def field(i):
        return meta_ref[:, i * tokens : (i + 1) * tokens]

    hit = jnp.zeros((count, tokens), jnp.float32)
    gate = jnp.zeros((count, tokens), jnp.float32)
    for k in range(top):
        named = (field(k) == expert).astype(jnp.float32)
        hit = hit + named
        gate = gate + named * field(top + k)
    row = lax.broadcasted_iota(jnp.int32, (tokens, tokens), 0)
    col = lax.broadcasted_iota(jnp.int32, (tokens, tokens), 1)
    earlier = ((row // tok_block == col // tok_block) & (row < col)).astype(jnp.float32)
    before = jnp.dot(hit, earlier, preferred_element_type=jnp.float32)
    block = lax.broadcasted_iota(jnp.int32, (count, tokens), 1) // tok_block
    place = jnp.where(hit > 0, block * capacity + before.astype(jnp.int32), -1)
    slot = lax.broadcasted_iota(jnp.int32, (slots, tokens), 0)
    for i in range(count):
        source = lax.rem(me + (count - i), count) if in_ring else i
        pick = (slot == place[i : i + 1]).astype(jnp.bfloat16)
        hid = hid_ref[:, source].reshape(slots, hid_ref.shape[-1])
        rows = lax.dot_general(hid, pick, (((0,), (0,)), ((), ())), preferred_element_type=jnp.float32)
        rows = (rows * gate[i : i + 1]).astype(jnp.bfloat16)
        at = pl.ds(pl.multiple_of(source * tokens, tokens), tokens)
        rows_ref[:, :, at] = rows.reshape(rows_ref.shape[0], rows_ref.shape[1], tokens)
    for masks, out in zip(groups, outs):
        for i, mask in enumerate(masks):
            out[i] = rows_ref[section ^ mask]


def token_acts(metas, hidden, groups, top, tok_block, in_ring):
    sections = lax.axis_size("section")
    mb_count, count, capacity, ff_width = hidden.shape
    rows = ff_width // sections
    depth = count * metas.shape[1] // (2 * top)
    return pl.pallas_call(
        partial(token_acts_kernel, groups=groups, top=top, capacity=capacity, tok_block=tok_block, in_ring=in_ring),
        in_specs=[pl.BlockSpec(memory_space=pltpu.VMEM)] * 2,
        out_specs=[pl.BlockSpec(memory_space=pltpu.VMEM)] * len(groups),
        out_shape=[jax.ShapeDtypeStruct((len(masks), rows, depth), jnp.bfloat16) for masks in groups],
        scratch_shapes=[pltpu.VMEM((sections, rows, depth), jnp.bfloat16)],
        compiler_params=pltpu.CompilerParams(vmem_limit_bytes=VMEM),
        cost_estimate=SHORT,
    )(metas, hidden)


def product_kernel(own_ref, mirror_ref, *refs, tokens, layout):
    count, rows, depth = own_ref.shape
    cots, outs, packed = refs[: -1 - count], refs[-1 - count : -1], refs[-1]
    sources = depth // tokens
    me = lax.axis_index("expert")
    for cot, (behind, replica) in zip(cots, layout):
        for i in range(cot.shape[0]):
            source = i if behind is None else lax.rem(me + (sources - behind), sources)
            for part in range(cot.shape[1] // tokens):
                start = pl.multiple_of(source * tokens + (replica + part) * depth, tokens)
                packed[pl.ds(start, tokens)] = cot[i, part * tokens : (part + 1) * tokens]
    own = jnp.dot(own_ref[...].reshape(count * rows, depth), packed[:depth], preferred_element_type=jnp.float32)
    mirror = jnp.dot(mirror_ref[...].reshape(count * rows, depth), packed[depth:], preferred_element_type=jnp.float32)
    for i, out in enumerate(outs):
        j = count - 1 - i
        total = own[i * rows : (i + 1) * rows] + mirror[j * rows : (j + 1) * rows]
        out[...] = total.astype(jnp.bfloat16)


def product(own_acts, mirror_acts, cots, layout, tokens, tile):
    count, rows, depth = own_acts.shape
    width = cots[0].shape[-1]
    acts_spec = pl.BlockSpec((count, rows, depth), lambda n: (0, 0, 0))
    return pl.pallas_call(
        partial(product_kernel, tokens=tokens, layout=layout),
        grid=(width // tile,),
        in_specs=[acts_spec, acts_spec] + [pl.BlockSpec((*cot.shape[:2], tile), lambda n: (0, 0, n)) for cot in cots],
        out_specs=[pl.BlockSpec((rows, tile), lambda n: (0, n))] * count,
        out_shape=[jax.ShapeDtypeStruct((rows, width), jnp.bfloat16)] * count,
        scratch_shapes=[pltpu.VMEM((2 * depth, tile), jnp.bfloat16)],
        compiler_params=pltpu.CompilerParams(vmem_limit_bytes=VMEM),
        cost_estimate=SHORT,
    )(own_acts, mirror_acts, *cots)


def tile_of(width):
    return next((width // parts for parts in (3, 2) if width % (128 * parts) == 0), width)


def join_kernel(*refs, masks, sections, offset):
    pieces = refs[: len(masks)]
    out, sem = refs[-2:]
    section = lax.axis_index("section")
    width = pieces[0].shape[-1]
    copies = []
    for i, (mask, piece) in enumerate(zip(masks, pieces)):
        source = section ^ mask
        upper = (source >= sections // 2).astype(jnp.int32)
        pair = source + upper * (sections - 1 - 2 * source)
        column = pl.multiple_of(upper * (out.shape[-1] // 2) + offset, 128)
        copies.append(pltpu.make_async_copy(piece, out.at[pair, 0, :, pl.ds(column, width)], sem.at[i]))
    for copy in copies:
        copy.start()
    for copy in copies:
        copy.wait()


def join(pieces, masks, sections, offset, half_width, out=None):
    rows = pieces[0].shape[0]
    shape = jax.ShapeDtypeStruct((sections // 2, 1, rows, 2 * half_width), jnp.bfloat16)
    first = out is None
    operands = tuple(pieces) if first else (*pieces, out)
    return pl.pallas_call(
        partial(join_kernel, masks=masks, sections=sections, offset=offset),
        in_specs=[pl.BlockSpec(memory_space=pltpu.VMEM)] * len(masks) + [pl.BlockSpec(memory_space=pl.ANY)] * (not first),
        out_specs=pl.BlockSpec(memory_space=pl.ANY),
        out_shape=shape,
        scratch_shapes=[pltpu.SemaphoreType.DMA((len(masks),))],
        input_output_aliases={} if first else {len(masks): 0},
        compiler_params=pltpu.CompilerParams(vmem_limit_bytes=VMEM),
    )(*operands)


def shift(block, axis, size, step):
    return lax.ppermute(block, axis, [(i, (i + step) % size) for i in range(size)])


def ring(block, axis, size):
    return [block] + [shift(block, axis, size, step) for step in range(1, size)]


def pass_on(own, first, back, axis):
    me = lax.axis_index(axis)
    chosen = jnp.where(me == 2, first, jnp.where(me == 1, back, own))
    return lax.ppermute(chosen, axis, [(0, 2), (2, 3), (3, 1), (1, 0)])


def repeat_kernel(*refs):
    blocks, out = refs[:-2], refs[-1]
    at = 0
    for block in blocks:
        out[0, at : at + block.shape[0]] = block[...]
        at += block.shape[0]


def repeat(blocks, after, count):
    rows, width = sum(block.shape[0] for block in blocks), blocks[0].shape[1]
    return pl.pallas_call(
        repeat_kernel,
        grid=(count,),
        in_specs=[pl.BlockSpec(block.shape, lambda i: (0, 0)) for block in blocks] + [pl.BlockSpec(memory_space=pl.ANY)],
        out_specs=pl.BlockSpec((1, rows, width), lambda i: (i, 0, 0)),
        out_shape=jax.ShapeDtypeStruct((count, rows, width), blocks[0].dtype),
        compiler_params=pltpu.CompilerParams(vmem_limit_bytes=VMEM),
        cost_estimate=LONG,
    )(*blocks, after)


def local(cotangent, routes, gate_prob, hidden):
    n_section = lax.axis_size("section")
    n_expert = lax.axis_size("expert")
    section = lax.axis_index("section")
    expert = lax.axis_index("expert")
    mb_count = hidden.shape[2]
    tokens, width = cotangent.shape[1:]
    top = routes.shape[2]
    half_width = width // 2
    widths = [half_width * 5 // 8, half_width * 3 // 8]
    offsets = [sum(widths[:c]) for c in range(len(widths))]
    mirror = [(i, n_section - 1 - i) for i in range(n_section)]
    upper = section >= n_section // 2
    quarter = n_section // 4
    near = [start + i for i in range(quarter // 2) for start in (quarter, 2 * quarter)]
    near += [n_section - 1 - mask for mask in reversed(near)]
    groups = [[mask for mask in range(n_section) if mask not in near], near]
    short = n_expert == 4
    meta = jnp.concatenate([routes[0].astype(jnp.float32), gate_prob[0]], 1).T.reshape(-1)
    metas = jnp.stack(ring(meta, "expert", n_expert)) if short else lax.all_gather(meta, "expert")
    acts = token_acts(metas, hidden[0, 0], groups, top, tokens // mb_count, short)
    cot = cotangent[0]
    kept, given = [], []
    for offset, span in zip(offsets, widths):
        low = cot[:, offset : offset + span]
        high = cot[:, half_width + offset : half_width + offset + span]
        kept.append(jnp.where(upper, high, low))
        given.append(jnp.where(upper, low, high))
    taken = lax.ppermute(jnp.concatenate(given, 1), "section", mirror)
    taken = [taken[:, offset : offset + span] for offset, span in zip(offsets, widths)]
    if short:
        kept_first = shift(kept[0], "expert", n_expert, 1)
        *held, _ = lax.optimization_barrier((*acts, taken[0]))
        mirror_acts = [lax.ppermute(group, "section", mirror) for group in held]
        kept_back = shift(kept[0], "expert", n_expert, 3)
        kept_passed = pass_on(kept[0], kept_first, kept_back, "expert")
        taken_first, taken_back = shift(taken[0], "expert", n_expert, 1), shift(taken[0], "expert", n_expert, 3)
        taken_first, taken_back, mirror_acts[0] = lax.optimization_barrier((taken_first, taken_back, mirror_acts[0]))
        taken_passed = pass_on(taken[0], taken_first, taken_back, "expert")
        kept_passed, taken_passed, mirror_acts[1] = lax.optimization_barrier(
            (kept_passed, taken_passed, mirror_acts[1])
        )
        later = repeat([kept[1], taken[1]], taken_first, n_expert)
        later, taken_passed = lax.optimization_barrier((later, taken_passed))
        later = lax.all_to_all(later, "expert", split_axis=0, concat_axis=0, tiled=True)
        blocks = [kept[0], kept_first, kept_passed, kept_back, taken[0], taken_first, taken_passed, taken_back]
        cots = [[block[None] for block in blocks], [later]]
        layouts = [[(step, replica) for replica in range(2) for step in range(n_expert)], [(None, 0)]]
    else:
        mirror_acts = [lax.ppermute(group, "section", mirror) for group in acts]
        cots = [[lax.all_gather(jnp.concatenate([a, b]), "expert")] for a, b in zip(kept, taken)]
        layouts = [[(None, 0)]] * len(cots)

    out = None
    for c, (offset, span) in enumerate(zip(offsets, widths)):
        pieces = [None] * n_section
        for g, masks in enumerate(groups):
            sums = list(product(acts[g], mirror_acts[g], cots[c], layouts[c], tokens, tile_of(span)))
            for mask, rows in zip(masks, sums):
                pieces[mask] = rows
                if mask:
                    pieces[mask] = lax.ppermute(rows, "section", [(i, i ^ mask) for i in range(n_section)])
        if c == 0:
            sent = [1, near[0], near[1], n_section - 2]
            early, cots[c + 1] = lax.optimization_barrier(([pieces[mask] for mask in sent], cots[c + 1]))
            for mask, rows in zip(sent, early):
                pieces[mask] = rows
        out = join(pieces, list(range(n_section)), n_section, offset, half_width, out)
    return out


def solution(mesh):
    return jax.shard_map(
        local,
        mesh=mesh,
        in_specs=(
            P("section", "expert", None),
            P("section", "expert", None),
            P("section", "expert", None),
            P("section", "expert", None, None, None),
        ),
        out_specs=P(None, "expert", "section", None),
        check_vma=False,
    )
```

```python
from functools import partial

import jax
import jax.numpy as jnp
from jax import lax
from jax.experimental import pallas as pl
from jax.experimental.pallas import tpu as pltpu
from jax.sharding import PartitionSpec as P

VMEM = 60 * 1024 * 1024
LONG = pl.CostEstimate(flops=10**11, bytes_accessed=10**6, transcendentals=0)
SHORT = pl.CostEstimate(flops=10**6, bytes_accessed=10**3, transcendentals=0)


def token_acts_kernel(meta_ref, hid_ref, *refs, groups, top, capacity, tok_block, in_ring):
    outs, rows_ref = refs[:-1], refs[-1]
    count = hid_ref.shape[1]
    tokens = rows_ref.shape[-1] // count
    slots = hid_ref.shape[0] * hid_ref.shape[2]
    me, section = lax.axis_index("expert"), lax.axis_index("section")
    expert = me.astype(jnp.float32)

    def field(i):
        return meta_ref[:, i * tokens : (i + 1) * tokens]

    hit = jnp.zeros((count, tokens), jnp.float32)
    gate = jnp.zeros((count, tokens), jnp.float32)
    for k in range(top):
        named = (field(k) == expert).astype(jnp.float32)
        hit = hit + named
        gate = gate + named * field(top + k)
    row = lax.broadcasted_iota(jnp.int32, (tokens, tokens), 0)
    col = lax.broadcasted_iota(jnp.int32, (tokens, tokens), 1)
    earlier = ((row // tok_block == col // tok_block) & (row < col)).astype(jnp.float32)
    before = jnp.dot(hit, earlier, preferred_element_type=jnp.float32)
    block = lax.broadcasted_iota(jnp.int32, (count, tokens), 1) // tok_block
    place = jnp.where(hit > 0, block * capacity + before.astype(jnp.int32), -1)
    slot = lax.broadcasted_iota(jnp.int32, (slots, tokens), 0)
    for i in range(count):
        source = lax.rem(me + (count - i), count) if in_ring else i
        pick = (slot == place[i : i + 1]).astype(jnp.bfloat16)
        hid = hid_ref[:, source].reshape(slots, hid_ref.shape[-1])
        rows = lax.dot_general(hid, pick, (((0,), (0,)), ((), ())), preferred_element_type=jnp.float32)
        rows = (rows * gate[i : i + 1]).astype(jnp.bfloat16)
        at = pl.ds(pl.multiple_of(source * tokens, tokens), tokens)
        rows_ref[:, :, at] = rows.reshape(rows_ref.shape[0], rows_ref.shape[1], tokens)
    for masks, out in zip(groups, outs):
        for i, mask in enumerate(masks):
            out[i] = rows_ref[section ^ mask]


def token_acts(metas, hidden, groups, top, tok_block, in_ring):
    sections = lax.axis_size("section")
    mb_count, count, capacity, ff_width = hidden.shape
    rows = ff_width // sections
    depth = count * metas.shape[1] // (2 * top)
    return pl.pallas_call(
        partial(token_acts_kernel, groups=groups, top=top, capacity=capacity, tok_block=tok_block, in_ring=in_ring),
        in_specs=[pl.BlockSpec(memory_space=pltpu.VMEM)] * 2,
        out_specs=[pl.BlockSpec(memory_space=pltpu.VMEM)] * len(groups),
        out_shape=[jax.ShapeDtypeStruct((len(masks), rows, depth), jnp.bfloat16) for masks in groups],
        scratch_shapes=[pltpu.VMEM((sections, rows, depth), jnp.bfloat16)],
        compiler_params=pltpu.CompilerParams(vmem_limit_bytes=VMEM),
        cost_estimate=SHORT,
    )(metas, hidden)


def product_kernel(own_ref, mirror_ref, *refs, tokens, layout):
    count, rows, depth = own_ref.shape
    cots, outs, packed = refs[: -1 - count], refs[-1 - count : -1], refs[-1]
    sources = depth // tokens
    me = lax.axis_index("expert")
    for cot, (behind, replica) in zip(cots, layout):
        for i in range(cot.shape[0]):
            source = i if behind is None else lax.rem(me + (sources - behind), sources)
            for part in range(cot.shape[1] // tokens):
                start = pl.multiple_of(source * tokens + (replica + part) * depth, tokens)
                packed[pl.ds(start, tokens)] = cot[i, part * tokens : (part + 1) * tokens]
    own = jnp.dot(own_ref[...].reshape(count * rows, depth), packed[:depth], preferred_element_type=jnp.float32)
    mirror = jnp.dot(mirror_ref[...].reshape(count * rows, depth), packed[depth:], preferred_element_type=jnp.float32)
    for i, out in enumerate(outs):
        j = i ^ 1
        total = own[i * rows : (i + 1) * rows] + mirror[j * rows : (j + 1) * rows]
        out[...] = total.astype(jnp.bfloat16)


def product(own_acts, mirror_acts, cots, layout, tokens, tile, part, parts):
    masks, rows, depth = own_acts.shape
    count = masks // parts
    width = cots[0].shape[-1]
    acts_spec = pl.BlockSpec((count, rows, depth), lambda n: (part, 0, 0))
    return pl.pallas_call(
        partial(product_kernel, tokens=tokens, layout=layout),
        grid=(width // tile,),
        in_specs=[acts_spec, acts_spec] + [pl.BlockSpec((*cot.shape[:2], tile), lambda n: (0, 0, n)) for cot in cots],
        out_specs=[pl.BlockSpec((rows, tile), lambda n: (0, n))] * count,
        out_shape=[jax.ShapeDtypeStruct((rows, width), jnp.bfloat16)] * count,
        scratch_shapes=[pltpu.VMEM((2 * depth, tile), jnp.bfloat16)],
        compiler_params=pltpu.CompilerParams(vmem_limit_bytes=VMEM),
        cost_estimate=SHORT,
    )(own_acts, mirror_acts, *cots)


def tile_of(width):
    return next((width // parts for parts in (3, 2) if width % (128 * parts) == 0), width)


def join_kernel(*refs, masks, sections, offset):
    pieces = refs[: len(masks)]
    out, sem = refs[-2:]
    section = lax.axis_index("section")
    width = pieces[0].shape[-1]
    copies = []
    for i, (mask, piece) in enumerate(zip(masks, pieces)):
        source = section ^ mask
        upper = (source >= sections // 2).astype(jnp.int32)
        pair = source + upper * (sections - 1 - 2 * source)
        column = pl.multiple_of(upper * (out.shape[-1] // 2) + offset, 128)
        copies.append(pltpu.make_async_copy(piece, out.at[pair, 0, :, pl.ds(column, width)], sem.at[i]))
    for copy in copies:
        copy.start()
    for copy in copies:
        copy.wait()


def join(pieces, masks, sections, offset, half_width, out=None):
    rows = pieces[0].shape[0]
    shape = jax.ShapeDtypeStruct((sections // 2, 1, rows, 2 * half_width), jnp.bfloat16)
    first = out is None
    operands = tuple(pieces) if first else (*pieces, out)
    return pl.pallas_call(
        partial(join_kernel, masks=masks, sections=sections, offset=offset),
        in_specs=[pl.BlockSpec(memory_space=pltpu.VMEM)] * len(masks) + [pl.BlockSpec(memory_space=pl.ANY)] * (not first),
        out_specs=pl.BlockSpec(memory_space=pl.ANY),
        out_shape=shape,
        scratch_shapes=[pltpu.SemaphoreType.DMA((len(masks),))],
        input_output_aliases={} if first else {len(masks): 0},
        compiler_params=pltpu.CompilerParams(vmem_limit_bytes=VMEM),
    )(*operands)


def shift(block, axis, size, step):
    return lax.ppermute(block, axis, [(i, (i + step) % size) for i in range(size)])


def ring(block, axis, size):
    return [block] + [shift(block, axis, size, step) for step in range(1, size)]


def pass_on(own, first, back, axis):
    me = lax.axis_index(axis)
    chosen = jnp.where(me == 2, first, jnp.where(me == 1, back, own))
    return lax.ppermute(chosen, axis, [(0, 2), (2, 3), (3, 1), (1, 0)])


def repeat_kernel(*refs):
    blocks, out = refs[:-2], refs[-1]
    at = 0
    for block in blocks:
        out[0, at : at + block.shape[0]] = block[...]
        at += block.shape[0]


def repeat(blocks, after, count):
    rows, width = sum(block.shape[0] for block in blocks), blocks[0].shape[1]
    return pl.pallas_call(
        repeat_kernel,
        grid=(count,),
        in_specs=[pl.BlockSpec(block.shape, lambda i: (0, 0)) for block in blocks] + [pl.BlockSpec(memory_space=pl.ANY)],
        out_specs=pl.BlockSpec((1, rows, width), lambda i: (i, 0, 0)),
        out_shape=jax.ShapeDtypeStruct((count, rows, width), blocks[0].dtype),
        compiler_params=pltpu.CompilerParams(vmem_limit_bytes=VMEM),
        cost_estimate=LONG,
    )(*blocks, after)


def local(cotangent, routes, gate_prob, hidden):
    n_section = lax.axis_size("section")
    n_expert = lax.axis_size("expert")
    section = lax.axis_index("section")
    expert = lax.axis_index("expert")
    mb_count = hidden.shape[2]
    tokens, width = cotangent.shape[1:]
    top = routes.shape[2]
    half_width = width // 2
    widths = [half_width * 5 // 8, half_width * 3 // 8]
    offsets = [sum(widths[:c]) for c in range(len(widths))]
    mirror = [(i, n_section - 1 - i) for i in range(n_section)]
    upper = section >= n_section // 2
    quarter = n_section // 4
    near, far = [], []
    for i in range(quarter // 2):
        near += [quarter + i, n_section - 1 - quarter - i, 2 * quarter + i, n_section - 1 - 2 * quarter - i]
    for i in range(quarter):
        far += [i, n_section - 1 - i]
    groups = [far, near]
    short = n_expert == 4
    cot = cotangent[0]
    given = jnp.where(upper, cot[:, :half_width], cot[:, half_width:])
    cot, given = lax.optimization_barrier((cot, given))
    kept = jnp.where(upper, cot[:, half_width:], cot[:, :half_width])
    kept, routes, gate_prob = lax.optimization_barrier((kept, routes, gate_prob))
    kept = [kept[:, offset : offset + span] for offset, span in zip(offsets, widths)]
    meta = jnp.concatenate([routes[0].astype(jnp.float32), gate_prob[0]], 1).T.reshape(-1)
    metas = jnp.stack(ring(meta, "expert", n_expert)) if short else lax.all_gather(meta, "expert")
    acts = token_acts(metas, hidden[0, 0], groups, top, tokens // mb_count, short)
    taken = lax.ppermute(given, "section", mirror)
    taken = [taken[:, offset : offset + span] for offset, span in zip(offsets, widths)]
    if short:
        kept_first = shift(kept[0], "expert", n_expert, 1)
        *held, _ = lax.optimization_barrier((*acts, taken[0]))
        mirror_acts = [lax.ppermute(group, "section", mirror) for group in held]
        kept_back = shift(kept[0], "expert", n_expert, 3)
        kept_passed = pass_on(kept[0], kept_first, kept_back, "expert")
        taken_first, taken_back = shift(taken[0], "expert", n_expert, 1), shift(taken[0], "expert", n_expert, 3)
        taken_first, taken_back, mirror_acts[0] = lax.optimization_barrier((taken_first, taken_back, mirror_acts[0]))
        taken_passed = pass_on(taken[0], taken_first, taken_back, "expert")
        kept_passed, taken_passed, mirror_acts[1] = lax.optimization_barrier(
            (kept_passed, taken_passed, mirror_acts[1])
        )
        later = repeat([kept[1], taken[1]], taken_first, n_expert)
        later, taken_passed = lax.optimization_barrier((later, taken_passed))
        later = lax.all_to_all(later, "expert", split_axis=0, concat_axis=0, tiled=True)
        blocks = [kept[0], kept_first, kept_passed, kept_back, taken[0], taken_first, taken_passed, taken_back]
        cots = [[block[None] for block in blocks], [later]]
        layouts = [[(step, replica) for replica in range(2) for step in range(n_expert)], [(None, 0)]]
    else:
        mirror_acts = [lax.ppermute(group, "section", mirror) for group in acts]
        cots = [[lax.all_gather(jnp.concatenate([a, b]), "expert")] for a, b in zip(kept, taken)]
        layouts = [[(None, 0)]] * len(cots)

    out = None
    for c, (offset, span) in enumerate(zip(offsets, widths)):
        pieces = [None] * n_section
        for g, masks in enumerate(groups):
            parts = 2 if c == 0 else 1
            sums = []
            for part in range(parts):
                sums += product(acts[g], mirror_acts[g], cots[c], layouts[c], tokens, tile_of(span), part, parts)
            for mask, rows in zip(masks, sums):
                pieces[mask] = rows
                if mask:
                    pieces[mask] = lax.ppermute(rows, "section", [(i, i ^ mask) for i in range(n_section)])
        if c == 0:
            sent = [1, near[0], near[1], n_section - 2]
            early, cots[c + 1] = lax.optimization_barrier(([pieces[mask] for mask in sent], cots[c + 1]))
            for mask, rows in zip(sent, early):
                pieces[mask] = rows
        out = join(pieces, list(range(n_section)), n_section, offset, half_width, out)
    return out


def solution(mesh):
    return jax.shard_map(
        local,
        mesh=mesh,
        in_specs=(
            P("section", "expert", None),
            P("section", "expert", None),
            P("section", "expert", None),
            P("section", "expert", None, None, None),
        ),
        out_specs=P(None, "expert", "section", None),
        check_vma=False,
    )
```

```python
from functools import partial

import jax
import jax.numpy as jnp
from jax import lax
from jax.experimental import pallas as pl
from jax.experimental.pallas import tpu as pltpu
from jax.sharding import PartitionSpec as P

VMEM = 60 * 1024 * 1024
LONG = pl.CostEstimate(flops=10**11, bytes_accessed=10**6, transcendentals=0)
SHORT = pl.CostEstimate(flops=10**6, bytes_accessed=10**3, transcendentals=0)


def token_acts_kernel(meta_ref, hid_ref, *refs, groups, top, capacity, tok_block, in_ring):
    outs, rows_ref = refs[:-1], refs[-1]
    count = hid_ref.shape[1]
    tokens = rows_ref.shape[-1] // count
    slots = hid_ref.shape[0] * hid_ref.shape[2]
    me, section = lax.axis_index("expert"), lax.axis_index("section")
    expert = me.astype(jnp.float32)

    def field(i):
        return meta_ref[:, i * tokens : (i + 1) * tokens]

    hit = jnp.zeros((count, tokens), jnp.float32)
    gate = jnp.zeros((count, tokens), jnp.float32)
    for k in range(top):
        named = (field(k) == expert).astype(jnp.float32)
        hit = hit + named
        gate = gate + named * field(top + k)
    row = lax.broadcasted_iota(jnp.int32, (tokens, tokens), 0)
    col = lax.broadcasted_iota(jnp.int32, (tokens, tokens), 1)
    earlier = ((row // tok_block == col // tok_block) & (row < col)).astype(jnp.float32)
    before = jnp.dot(hit, earlier, preferred_element_type=jnp.float32)
    block = lax.broadcasted_iota(jnp.int32, (count, tokens), 1) // tok_block
    place = jnp.where(hit > 0, block * capacity + before.astype(jnp.int32), -1)
    slot = lax.broadcasted_iota(jnp.int32, (slots, tokens), 0)
    for i in range(count):
        source = lax.rem(me + (count - i), count) if in_ring else i
        pick = (slot == place[i : i + 1]).astype(jnp.bfloat16)
        hid = hid_ref[:, source].reshape(slots, hid_ref.shape[-1])
        rows = lax.dot_general(hid, pick, (((0,), (0,)), ((), ())), preferred_element_type=jnp.float32)
        rows = (rows * gate[i : i + 1]).astype(jnp.bfloat16)
        at = pl.ds(pl.multiple_of(source * tokens, tokens), tokens)
        rows_ref[:, :, at] = rows.reshape(rows_ref.shape[0], rows_ref.shape[1], tokens)
    for masks, out in zip(groups, outs):
        for i, mask in enumerate(masks):
            out[i] = rows_ref[section ^ mask]


def token_acts(metas, hidden, groups, top, tok_block, in_ring):
    sections = lax.axis_size("section")
    mb_count, count, capacity, ff_width = hidden.shape
    rows = ff_width // sections
    depth = count * metas.shape[1] // (2 * top)
    return pl.pallas_call(
        partial(token_acts_kernel, groups=groups, top=top, capacity=capacity, tok_block=tok_block, in_ring=in_ring),
        in_specs=[pl.BlockSpec(memory_space=pltpu.VMEM)] * 2,
        out_specs=[pl.BlockSpec(memory_space=pltpu.VMEM)] * len(groups),
        out_shape=[jax.ShapeDtypeStruct((len(masks), rows, depth), jnp.bfloat16) for masks in groups],
        scratch_shapes=[pltpu.VMEM((sections, rows, depth), jnp.bfloat16)],
        compiler_params=pltpu.CompilerParams(vmem_limit_bytes=VMEM),
        cost_estimate=SHORT,
    )(metas, hidden)


def product_kernel(own_ref, mirror_ref, *refs, tokens, layout):
    count, rows, depth = own_ref.shape
    cots, outs, packed = refs[: -1 - count], refs[-1 - count : -1], refs[-1]
    sources = depth // tokens
    me = lax.axis_index("expert")
    for cot, (behind, replica) in zip(cots, layout):
        for i in range(cot.shape[0]):
            source = i if behind is None else lax.rem(me + (sources - behind), sources)
            for part in range(cot.shape[1] // tokens):
                start = pl.multiple_of(source * tokens + (replica + part) * depth, tokens)
                packed[pl.ds(start, tokens)] = cot[i, part * tokens : (part + 1) * tokens]
    own = jnp.dot(own_ref[...].reshape(count * rows, depth), packed[:depth], preferred_element_type=jnp.float32)
    mirror = jnp.dot(mirror_ref[...].reshape(count * rows, depth), packed[depth:], preferred_element_type=jnp.float32)
    for i, out in enumerate(outs):
        j = i ^ 1
        total = own[i * rows : (i + 1) * rows] + mirror[j * rows : (j + 1) * rows]
        out[...] = total.astype(jnp.bfloat16)


def product(own_acts, mirror_acts, cots, layout, tokens, tile, part, parts):
    masks, rows, depth = own_acts.shape
    count = masks // parts
    width = cots[0].shape[-1]
    acts_spec = pl.BlockSpec((count, rows, depth), lambda n: (part, 0, 0))
    return pl.pallas_call(
        partial(product_kernel, tokens=tokens, layout=layout),
        grid=(width // tile,),
        in_specs=[acts_spec, acts_spec] + [pl.BlockSpec((*cot.shape[:2], tile), lambda n: (0, 0, n)) for cot in cots],
        out_specs=[pl.BlockSpec((rows, tile), lambda n: (0, n))] * count,
        out_shape=[jax.ShapeDtypeStruct((rows, width), jnp.bfloat16)] * count,
        scratch_shapes=[pltpu.VMEM((2 * depth, tile), jnp.bfloat16)],
        compiler_params=pltpu.CompilerParams(vmem_limit_bytes=VMEM),
        cost_estimate=SHORT,
    )(own_acts, mirror_acts, *cots)


def tile_of(width):
    return next((width // parts for parts in (3, 2) if width % (128 * parts) == 0), width)


def join_kernel(*refs, masks, sections, offset):
    pieces = refs[: len(masks)]
    out, sem = refs[-2:]
    section = lax.axis_index("section")
    width = pieces[0].shape[-1]
    copies = []
    for i, (mask, piece) in enumerate(zip(masks, pieces)):
        source = section ^ mask
        upper = (source >= sections // 2).astype(jnp.int32)
        pair = source + upper * (sections - 1 - 2 * source)
        column = pl.multiple_of(upper * (out.shape[-1] // 2) + offset, 128)
        copies.append(pltpu.make_async_copy(piece, out.at[pair, 0, :, pl.ds(column, width)], sem.at[i]))
    for copy in copies:
        copy.start()
    for copy in copies:
        copy.wait()


def join(pieces, masks, sections, offset, half_width, out=None):
    rows = pieces[0].shape[0]
    shape = jax.ShapeDtypeStruct((sections // 2, 1, rows, 2 * half_width), jnp.bfloat16)
    first = out is None
    operands = tuple(pieces) if first else (*pieces, out)
    return pl.pallas_call(
        partial(join_kernel, masks=masks, sections=sections, offset=offset),
        in_specs=[pl.BlockSpec(memory_space=pltpu.VMEM)] * len(masks) + [pl.BlockSpec(memory_space=pl.ANY)] * (not first),
        out_specs=pl.BlockSpec(memory_space=pl.ANY),
        out_shape=shape,
        scratch_shapes=[pltpu.SemaphoreType.DMA((len(masks),))],
        input_output_aliases={} if first else {len(masks): 0},
        compiler_params=pltpu.CompilerParams(vmem_limit_bytes=VMEM),
    )(*operands)


def shift(block, axis, size, step):
    return lax.ppermute(block, axis, [(i, (i + step) % size) for i in range(size)])


def ring(block, axis, size):
    return [block] + [shift(block, axis, size, step) for step in range(1, size)]


def pass_on(own, first, back, axis):
    me = lax.axis_index(axis)
    chosen = jnp.where(me == 2, first, jnp.where(me == 1, back, own))
    return lax.ppermute(chosen, axis, [(0, 2), (2, 3), (3, 1), (1, 0)])


def repeat_kernel(*refs):
    blocks, out = refs[:-2], refs[-1]
    at = 0
    for block in blocks:
        out[0, at : at + block.shape[0]] = block[...]
        at += block.shape[0]


def repeat(blocks, after, count):
    rows, width = sum(block.shape[0] for block in blocks), blocks[0].shape[1]
    return pl.pallas_call(
        repeat_kernel,
        grid=(count,),
        in_specs=[pl.BlockSpec(block.shape, lambda i: (0, 0)) for block in blocks] + [pl.BlockSpec(memory_space=pl.ANY)],
        out_specs=pl.BlockSpec((1, rows, width), lambda i: (i, 0, 0)),
        out_shape=jax.ShapeDtypeStruct((count, rows, width), blocks[0].dtype),
        compiler_params=pltpu.CompilerParams(vmem_limit_bytes=VMEM),
        cost_estimate=LONG,
    )(*blocks, after)


def local(cotangent, routes, gate_prob, hidden):
    n_section = lax.axis_size("section")
    n_expert = lax.axis_size("expert")
    section = lax.axis_index("section")
    expert = lax.axis_index("expert")
    mb_count = hidden.shape[2]
    tokens, width = cotangent.shape[1:]
    top = routes.shape[2]
    half_width = width // 2
    widths = [half_width * 5 // 8, half_width * 3 // 8]
    offsets = [sum(widths[:c]) for c in range(len(widths))]
    mirror = [(i, n_section - 1 - i) for i in range(n_section)]
    upper = section >= n_section // 2
    quarter = n_section // 4
    near, far = [], []
    for i in range(quarter // 2):
        near += [quarter + i, n_section - 1 - quarter - i, 2 * quarter + i, n_section - 1 - 2 * quarter - i]
    for i in range(quarter):
        far += [i, n_section - 1 - i]
    groups = [far, near]
    short = n_expert == 4
    cot = cotangent[0]
    given = jnp.where(upper, cot[:, :half_width], cot[:, half_width:])
    cot, given = lax.optimization_barrier((cot, given))
    kept = jnp.where(upper, cot[:, half_width:], cot[:, :half_width])
    kept, routes, gate_prob = lax.optimization_barrier((kept, routes, gate_prob))
    kept = [kept[:, offset : offset + span] for offset, span in zip(offsets, widths)]
    meta = jnp.concatenate([routes[0].astype(jnp.float32), gate_prob[0]], 1).T.reshape(-1)
    metas = jnp.stack(ring(meta, "expert", n_expert)) if short else lax.all_gather(meta, "expert")
    acts = token_acts(metas, hidden[0, 0], groups, top, tokens // mb_count, short)
    taken = lax.ppermute(given, "section", mirror)
    taken = [taken[:, offset : offset + span] for offset, span in zip(offsets, widths)]
    if short:
        kept_first = shift(kept[0], "expert", n_expert, 1)
        *held, sent_back = lax.optimization_barrier((*acts, kept[0]))
        mirror_acts = [lax.ppermute(group, "section", mirror) for group in held]
        kept_back = shift(sent_back, "expert", n_expert, 3)
        kept_passed = pass_on(kept[0], kept_first, kept_back, "expert")
        taken_first, taken_back = shift(taken[0], "expert", n_expert, 1), shift(taken[0], "expert", n_expert, 3)
        taken_first, taken_back, mirror_acts[0] = lax.optimization_barrier((taken_first, taken_back, mirror_acts[0]))
        taken_passed = pass_on(taken[0], taken_first, taken_back, "expert")
        kept_passed, taken_passed, mirror_acts[1] = lax.optimization_barrier(
            (kept_passed, taken_passed, mirror_acts[1])
        )
        later = repeat([kept[1], taken[1]], taken_first, n_expert)
        later, taken_passed = lax.optimization_barrier((later, taken_passed))
        later = lax.all_to_all(later, "expert", split_axis=0, concat_axis=0, tiled=True)
        blocks = [kept[0], kept_first, kept_passed, kept_back, taken[0], taken_first, taken_passed, taken_back]
        cots = [[block[None] for block in blocks], [later]]
        layouts = [[(step, replica) for replica in range(2) for step in range(n_expert)], [(None, 0)]]
    else:
        mirror_acts = [lax.ppermute(group, "section", mirror) for group in acts]
        cots = [[lax.all_gather(jnp.concatenate([a, b]), "expert")] for a, b in zip(kept, taken)]
        layouts = [[(None, 0)]] * len(cots)

    out = None
    for c, (offset, span) in enumerate(zip(offsets, widths)):
        pieces = [None] * n_section
        for g, masks in enumerate(groups):
            parts = 2 if c == 0 else 1
            sums = []
            for part in range(parts):
                sums += product(acts[g], mirror_acts[g], cots[c], layouts[c], tokens, tile_of(span), part, parts)
            for mask, rows in zip(masks, sums):
                pieces[mask] = rows
                if mask:
                    pieces[mask] = lax.ppermute(rows, "section", [(i, i ^ mask) for i in range(n_section)])
        if c == 0:
            sent = [1, near[0], near[1], n_section - 2]
            early, cots[c + 1] = lax.optimization_barrier(([pieces[mask] for mask in sent], cots[c + 1]))
            for mask, rows in zip(sent, early):
                pieces[mask] = rows
        out = join(pieces, list(range(n_section)), n_section, offset, half_width, out)
    return out


def solution(mesh):
    return jax.shard_map(
        local,
        mesh=mesh,
        in_specs=(
            P("section", "expert", None),
            P("section", "expert", None),
            P("section", "expert", None),
            P("section", "expert", None, None, None),
        ),
        out_specs=P(None, "expert", "section", None),
        check_vma=False,
    )
```

```python
from functools import partial

import jax
import jax.numpy as jnp
from jax import lax
from jax.experimental import pallas as pl
from jax.experimental.pallas import tpu as pltpu
from jax.sharding import PartitionSpec as P

VMEM = 60 * 1024 * 1024
LONG = pl.CostEstimate(flops=10**11, bytes_accessed=10**6, transcendentals=0)
SHORT = pl.CostEstimate(flops=10**6, bytes_accessed=10**3, transcendentals=0)


def token_acts_kernel(meta_ref, hid_ref, *refs, groups, top, capacity, tok_block, in_ring):
    outs, rows_ref = refs[:-1], refs[-1]
    count = hid_ref.shape[1]
    tokens = rows_ref.shape[-1] // count
    slots = hid_ref.shape[0] * hid_ref.shape[2]
    me, section = lax.axis_index("expert"), lax.axis_index("section")
    expert = me.astype(jnp.float32)

    def field(i):
        return meta_ref[:, i * tokens : (i + 1) * tokens]

    hit = jnp.zeros((count, tokens), jnp.float32)
    gate = jnp.zeros((count, tokens), jnp.float32)
    for k in range(top):
        named = (field(k) == expert).astype(jnp.float32)
        hit = hit + named
        gate = gate + named * field(top + k)
    row = lax.broadcasted_iota(jnp.int32, (tokens, tokens), 0)
    col = lax.broadcasted_iota(jnp.int32, (tokens, tokens), 1)
    earlier = ((row // tok_block == col // tok_block) & (row < col)).astype(jnp.float32)
    before = jnp.dot(hit, earlier, preferred_element_type=jnp.float32)
    block = lax.broadcasted_iota(jnp.int32, (count, tokens), 1) // tok_block
    place = jnp.where(hit > 0, block * capacity + before.astype(jnp.int32), -1)
    slot = lax.broadcasted_iota(jnp.int32, (slots, tokens), 0)
    for i in range(count):
        source = lax.rem(me + (count - i), count) if in_ring else i
        pick = (slot == place[i : i + 1]).astype(jnp.bfloat16)
        hid = hid_ref[:, source].reshape(slots, hid_ref.shape[-1])
        rows = lax.dot_general(hid, pick, (((0,), (0,)), ((), ())), preferred_element_type=jnp.float32)
        rows = (rows * gate[i : i + 1]).astype(jnp.bfloat16)
        at = pl.ds(pl.multiple_of(source * tokens, tokens), tokens)
        rows_ref[:, :, at] = rows.reshape(rows_ref.shape[0], rows_ref.shape[1], tokens)
    for masks, out in zip(groups, outs):
        for i, mask in enumerate(masks):
            out[i] = rows_ref[section ^ mask]


def token_acts(metas, hidden, groups, top, tok_block, in_ring):
    sections = lax.axis_size("section")
    mb_count, count, capacity, ff_width = hidden.shape
    rows = ff_width // sections
    depth = count * metas.shape[1] // (2 * top)
    return pl.pallas_call(
        partial(token_acts_kernel, groups=groups, top=top, capacity=capacity, tok_block=tok_block, in_ring=in_ring),
        in_specs=[pl.BlockSpec(memory_space=pltpu.VMEM)] * 2,
        out_specs=[pl.BlockSpec(memory_space=pltpu.VMEM)] * len(groups),
        out_shape=[jax.ShapeDtypeStruct((len(masks), rows, depth), jnp.bfloat16) for masks in groups],
        scratch_shapes=[pltpu.VMEM((sections, rows, depth), jnp.bfloat16)],
        compiler_params=pltpu.CompilerParams(vmem_limit_bytes=VMEM),
        cost_estimate=SHORT,
    )(metas, hidden)


def product_kernel(own_ref, mirror_ref, *refs, tokens, layout):
    count, rows, depth = own_ref.shape
    cots, outs, packed = refs[: -1 - count], refs[-1 - count : -1], refs[-1]
    sources = depth // tokens
    me = lax.axis_index("expert")
    for cot, (behind, replica) in zip(cots, layout):
        for i in range(cot.shape[0]):
            source = i if behind is None else lax.rem(me + (sources - behind), sources)
            for part in range(cot.shape[1] // tokens):
                start = pl.multiple_of(source * tokens + (replica + part) * depth, tokens)
                packed[pl.ds(start, tokens)] = cot[i, part * tokens : (part + 1) * tokens]
    own = jnp.dot(own_ref[...].reshape(count * rows, depth), packed[:depth], preferred_element_type=jnp.float32)
    mirror = jnp.dot(mirror_ref[...].reshape(count * rows, depth), packed[depth:], preferred_element_type=jnp.float32)
    for i, out in enumerate(outs):
        j = i ^ 1
        total = own[i * rows : (i + 1) * rows] + mirror[j * rows : (j + 1) * rows]
        out[...] = total.astype(jnp.bfloat16)


def product(own_acts, mirror_acts, cots, layout, tokens, tile, part, parts):
    masks, rows, depth = own_acts.shape
    count = masks // parts
    width = cots[0].shape[-1]
    acts_spec = pl.BlockSpec((count, rows, depth), lambda n: (part, 0, 0))
    return pl.pallas_call(
        partial(product_kernel, tokens=tokens, layout=layout),
        grid=(width // tile,),
        in_specs=[acts_spec, acts_spec] + [pl.BlockSpec((*cot.shape[:2], tile), lambda n: (0, 0, n)) for cot in cots],
        out_specs=[pl.BlockSpec((rows, tile), lambda n: (0, n))] * count,
        out_shape=[jax.ShapeDtypeStruct((rows, width), jnp.bfloat16)] * count,
        scratch_shapes=[pltpu.VMEM((2 * depth, tile), jnp.bfloat16)],
        compiler_params=pltpu.CompilerParams(vmem_limit_bytes=VMEM),
        cost_estimate=SHORT,
    )(own_acts, mirror_acts, *cots)


def tile_of(width):
    return next((width // parts for parts in (3, 2) if width % (128 * parts) == 0), width)


def join_kernel(*refs, masks, sections, offset):
    pieces = refs[: len(masks)]
    out, sem = refs[-2:]
    section = lax.axis_index("section")
    width = pieces[0].shape[-1]
    copies = []
    for i, (mask, piece) in enumerate(zip(masks, pieces)):
        source = section ^ mask
        upper = (source >= sections // 2).astype(jnp.int32)
        pair = source + upper * (sections - 1 - 2 * source)
        column = pl.multiple_of(upper * (out.shape[-1] // 2) + offset, 128)
        copies.append(pltpu.make_async_copy(piece, out.at[pair, 0, :, pl.ds(column, width)], sem.at[i]))
    for copy in copies:
        copy.start()
    for copy in copies:
        copy.wait()


def join(pieces, masks, sections, offset, half_width, out=None):
    rows = pieces[0].shape[0]
    shape = jax.ShapeDtypeStruct((sections // 2, 1, rows, 2 * half_width), jnp.bfloat16)
    first = out is None
    operands = tuple(pieces) if first else (*pieces, out)
    return pl.pallas_call(
        partial(join_kernel, masks=masks, sections=sections, offset=offset),
        in_specs=[pl.BlockSpec(memory_space=pltpu.VMEM)] * len(masks) + [pl.BlockSpec(memory_space=pl.ANY)] * (not first),
        out_specs=pl.BlockSpec(memory_space=pl.ANY),
        out_shape=shape,
        scratch_shapes=[pltpu.SemaphoreType.DMA((len(masks),))],
        input_output_aliases={} if first else {len(masks): 0},
        compiler_params=pltpu.CompilerParams(vmem_limit_bytes=VMEM),
    )(*operands)


def shift(block, axis, size, step):
    return lax.ppermute(block, axis, [(i, (i + step) % size) for i in range(size)])


def ring(block, axis, size):
    return [block] + [shift(block, axis, size, step) for step in range(1, size)]


def pass_on(own, first, back, axis):
    me = lax.axis_index(axis)
    chosen = jnp.where(me == 2, first, jnp.where(me == 1, back, own))
    return lax.ppermute(chosen, axis, [(0, 2), (2, 3), (3, 1), (1, 0)])


def repeat_kernel(*refs):
    blocks, out = refs[:-2], refs[-1]
    at = 0
    for block in blocks:
        out[0, at : at + block.shape[0]] = block[...]
        at += block.shape[0]


def repeat(blocks, after, count):
    rows, width = sum(block.shape[0] for block in blocks), blocks[0].shape[1]
    return pl.pallas_call(
        repeat_kernel,
        grid=(count,),
        in_specs=[pl.BlockSpec(block.shape, lambda i: (0, 0)) for block in blocks] + [pl.BlockSpec(memory_space=pl.ANY)],
        out_specs=pl.BlockSpec((1, rows, width), lambda i: (i, 0, 0)),
        out_shape=jax.ShapeDtypeStruct((count, rows, width), blocks[0].dtype),
        compiler_params=pltpu.CompilerParams(vmem_limit_bytes=VMEM),
        cost_estimate=LONG,
    )(*blocks, after)


def local(cotangent, routes, gate_prob, hidden):
    n_section = lax.axis_size("section")
    n_expert = lax.axis_size("expert")
    section = lax.axis_index("section")
    expert = lax.axis_index("expert")
    mb_count = hidden.shape[2]
    tokens, width = cotangent.shape[1:]
    top = routes.shape[2]
    half_width = width // 2
    widths = [half_width * 5 // 8, half_width * 3 // 8]
    offsets = [sum(widths[:c]) for c in range(len(widths))]
    mirror = [(i, n_section - 1 - i) for i in range(n_section)]
    upper = section >= n_section // 2
    quarter = n_section // 4
    near, far = [], []
    for i in range(quarter // 2):
        near += [quarter + i, n_section - 1 - quarter - i, 2 * quarter + i, n_section - 1 - 2 * quarter - i]
    for i in range(quarter):
        far += [i, n_section - 1 - i]
    groups = [far, near]
    short = n_expert == 4
    cot = cotangent[0]
    given = lax.dynamic_slice_in_dim(cot, jnp.where(upper, 0, half_width), half_width, 1)
    cot, given = lax.optimization_barrier((cot, given))
    kept = lax.dynamic_slice_in_dim(cot, jnp.where(upper, half_width, 0), half_width, 1)
    kept, routes, gate_prob = lax.optimization_barrier((kept, routes, gate_prob))
    kept = [kept[:, offset : offset + span] for offset, span in zip(offsets, widths)]
    meta = jnp.concatenate([routes[0].astype(jnp.float32), gate_prob[0]], 1).T.reshape(-1)
    metas = jnp.stack(ring(meta, "expert", n_expert)) if short else lax.all_gather(meta, "expert")
    acts = token_acts(metas, hidden[0, 0], groups, top, tokens // mb_count, short)
    taken = lax.ppermute(given, "section", mirror)
    taken = [taken[:, offset : offset + span] for offset, span in zip(offsets, widths)]
    if short:
        kept_first = shift(kept[0], "expert", n_expert, 1)
        *held, sent_back = lax.optimization_barrier((*acts, kept[0]))
        mirror_acts = [lax.ppermute(group, "section", mirror) for group in held]
        kept_back = shift(sent_back, "expert", n_expert, 3)
        kept_passed = pass_on(kept[0], kept_first, kept_back, "expert")
        taken_first, taken_back = shift(taken[0], "expert", n_expert, 1), shift(taken[0], "expert", n_expert, 3)
        taken_first, taken_back, mirror_acts[0] = lax.optimization_barrier((taken_first, taken_back, mirror_acts[0]))
        taken_passed = pass_on(taken[0], taken_first, taken_back, "expert")
        kept_passed, taken_passed, mirror_acts[1] = lax.optimization_barrier(
            (kept_passed, taken_passed, mirror_acts[1])
        )
        later = repeat([kept[1], taken[1]], taken_first, n_expert)
        later, taken_passed = lax.optimization_barrier((later, taken_passed))
        later = lax.all_to_all(later, "expert", split_axis=0, concat_axis=0, tiled=True)
        blocks = [kept[0], kept_first, kept_passed, kept_back, taken[0], taken_first, taken_passed, taken_back]
        cots = [[block[None] for block in blocks], [later]]
        layouts = [[(step, replica) for replica in range(2) for step in range(n_expert)], [(None, 0)]]
    else:
        mirror_acts = [lax.ppermute(group, "section", mirror) for group in acts]
        cots = [[lax.all_gather(jnp.concatenate([a, b]), "expert")] for a, b in zip(kept, taken)]
        layouts = [[(None, 0)]] * len(cots)

    out = None
    for c, (offset, span) in enumerate(zip(offsets, widths)):
        pieces = [None] * n_section
        for g, masks in enumerate(groups):
            parts = 2 if c == 0 else 1
            sums = []
            for part in range(parts):
                sums += product(acts[g], mirror_acts[g], cots[c], layouts[c], tokens, tile_of(span), part, parts)
            for mask, rows in zip(masks, sums):
                pieces[mask] = rows
                if mask:
                    pieces[mask] = lax.ppermute(rows, "section", [(i, i ^ mask) for i in range(n_section)])
        if c == 0:
            sent = [1, near[0], near[1], n_section - 2]
            early, cots[c + 1] = lax.optimization_barrier(([pieces[mask] for mask in sent], cots[c + 1]))
            for mask, rows in zip(sent, early):
                pieces[mask] = rows
        out = join(pieces, list(range(n_section)), n_section, offset, half_width, out)
    return out


def solution(mesh):
    return jax.shard_map(
        local,
        mesh=mesh,
        in_specs=(
            P("section", "expert", None),
            P("section", "expert", None),
            P("section", "expert", None),
            P("section", "expert", None, None, None),
        ),
        out_specs=P(None, "expert", "section", None),
        check_vma=False,
    )
```

```python
from functools import partial

import jax
import jax.numpy as jnp
from jax import lax
from jax.experimental import pallas as pl
from jax.experimental.pallas import tpu as pltpu
from jax.sharding import PartitionSpec as P

VMEM = 60 * 1024 * 1024
LONG = pl.CostEstimate(flops=10**11, bytes_accessed=10**6, transcendentals=0)
SHORT = pl.CostEstimate(flops=10**6, bytes_accessed=10**3, transcendentals=0)


def token_acts_kernel(meta_ref, hid_ref, *refs, groups, top, capacity, tok_block, in_ring):
    outs, rows_ref = refs[:-1], refs[-1]
    count = hid_ref.shape[1]
    tokens = rows_ref.shape[-1] // count
    slots = hid_ref.shape[0] * hid_ref.shape[2]
    me, section = lax.axis_index("expert"), lax.axis_index("section")
    expert = me.astype(jnp.float32)

    def field(i):
        return meta_ref[:, i * tokens : (i + 1) * tokens]

    hit = jnp.zeros((count, tokens), jnp.float32)
    gate = jnp.zeros((count, tokens), jnp.float32)
    for k in range(top):
        named = (field(k) == expert).astype(jnp.float32)
        hit = hit + named
        gate = gate + named * field(top + k)
    row = lax.broadcasted_iota(jnp.int32, (tokens, tokens), 0)
    col = lax.broadcasted_iota(jnp.int32, (tokens, tokens), 1)
    earlier = ((row // tok_block == col // tok_block) & (row < col)).astype(jnp.float32)
    before = jnp.dot(hit, earlier, preferred_element_type=jnp.float32)
    block = lax.broadcasted_iota(jnp.int32, (count, tokens), 1) // tok_block
    place = jnp.where(hit > 0, block * capacity + before.astype(jnp.int32), -1)
    slot = lax.broadcasted_iota(jnp.int32, (slots, tokens), 0)
    for i in range(count):
        source = lax.rem(me + (count - i), count) if in_ring else i
        pick = (slot == place[i : i + 1]).astype(jnp.bfloat16)
        hid = hid_ref[:, source].reshape(slots, hid_ref.shape[-1])
        rows = lax.dot_general(hid, pick, (((0,), (0,)), ((), ())), preferred_element_type=jnp.float32)
        rows = (rows * gate[i : i + 1]).astype(jnp.bfloat16)
        at = pl.ds(pl.multiple_of(source * tokens, tokens), tokens)
        rows_ref[:, :, at] = rows.reshape(rows_ref.shape[0], rows_ref.shape[1], tokens)
    for masks, out in zip(groups, outs):
        for i, mask in enumerate(masks):
            out[i] = rows_ref[section ^ mask]


def token_acts(metas, hidden, groups, top, tok_block, in_ring):
    sections = lax.axis_size("section")
    mb_count, count, capacity, ff_width = hidden.shape
    rows = ff_width // sections
    depth = count * metas.shape[1] // (2 * top)
    return pl.pallas_call(
        partial(token_acts_kernel, groups=groups, top=top, capacity=capacity, tok_block=tok_block, in_ring=in_ring),
        in_specs=[pl.BlockSpec(memory_space=pltpu.VMEM)] * 2,
        out_specs=[pl.BlockSpec(memory_space=pltpu.VMEM)] * len(groups),
        out_shape=[jax.ShapeDtypeStruct((len(masks), rows, depth), jnp.bfloat16) for masks in groups],
        scratch_shapes=[pltpu.VMEM((sections, rows, depth), jnp.bfloat16)],
        compiler_params=pltpu.CompilerParams(vmem_limit_bytes=VMEM),
        cost_estimate=SHORT,
    )(metas, hidden)


def product_kernel(own_ref, mirror_ref, *refs, tokens, layout):
    count, rows, depth = own_ref.shape
    cots, outs, packed = refs[: -1 - count], refs[-1 - count : -1], refs[-1]
    sources = depth // tokens
    me = lax.axis_index("expert")
    for cot, (behind, replica) in zip(cots, layout):
        for i in range(cot.shape[0]):
            source = i if behind is None else lax.rem(me + (sources - behind), sources)
            for part in range(cot.shape[1] // tokens):
                start = pl.multiple_of(source * tokens + (replica + part) * depth, tokens)
                packed[pl.ds(start, tokens)] = cot[i, part * tokens : (part + 1) * tokens]
    own = jnp.dot(own_ref[...].reshape(count * rows, depth), packed[:depth], preferred_element_type=jnp.float32)
    mirror = jnp.dot(mirror_ref[...].reshape(count * rows, depth), packed[depth:], preferred_element_type=jnp.float32)
    for i, out in enumerate(outs):
        j = i ^ 1
        total = own[i * rows : (i + 1) * rows] + mirror[j * rows : (j + 1) * rows]
        out[...] = total.astype(jnp.bfloat16)


def product(own_acts, mirror_acts, cots, layout, tokens, tile, part, parts):
    masks, rows, depth = own_acts.shape
    count = masks // parts
    width = cots[0].shape[-1]
    acts_spec = pl.BlockSpec((count, rows, depth), lambda n: (part, 0, 0))
    return pl.pallas_call(
        partial(product_kernel, tokens=tokens, layout=layout),
        grid=(width // tile,),
        in_specs=[acts_spec, acts_spec] + [pl.BlockSpec((*cot.shape[:2], tile), lambda n: (0, 0, n)) for cot in cots],
        out_specs=[pl.BlockSpec((rows, tile), lambda n: (0, n))] * count,
        out_shape=[jax.ShapeDtypeStruct((rows, width), jnp.bfloat16)] * count,
        scratch_shapes=[pltpu.VMEM((2 * depth, tile), jnp.bfloat16)],
        compiler_params=pltpu.CompilerParams(vmem_limit_bytes=VMEM),
        cost_estimate=SHORT,
    )(own_acts, mirror_acts, *cots)


def tile_of(width):
    return next((width // parts for parts in (3, 2) if width % (128 * parts) == 0), width)


def join_kernel(*refs, masks, sections, offset):
    pieces = refs[: len(masks)]
    out, sem = refs[-2:]
    section = lax.axis_index("section")
    width = pieces[0].shape[-1]
    copies = []
    for i, (mask, piece) in enumerate(zip(masks, pieces)):
        source = section ^ mask
        upper = (source >= sections // 2).astype(jnp.int32)
        pair = source + upper * (sections - 1 - 2 * source)
        column = pl.multiple_of(upper * (out.shape[-1] // 2) + offset, 128)
        copies.append(pltpu.make_async_copy(piece, out.at[pair, 0, :, pl.ds(column, width)], sem.at[i]))
    for copy in copies:
        copy.start()
    for copy in copies:
        copy.wait()


def join(pieces, masks, sections, offset, half_width, out=None):
    rows = pieces[0].shape[0]
    shape = jax.ShapeDtypeStruct((sections // 2, 1, rows, 2 * half_width), jnp.bfloat16)
    first = out is None
    operands = tuple(pieces) if first else (*pieces, out)
    return pl.pallas_call(
        partial(join_kernel, masks=masks, sections=sections, offset=offset),
        in_specs=[pl.BlockSpec(memory_space=pltpu.VMEM)] * len(masks) + [pl.BlockSpec(memory_space=pl.ANY)] * (not first),
        out_specs=pl.BlockSpec(memory_space=pl.ANY),
        out_shape=shape,
        scratch_shapes=[pltpu.SemaphoreType.DMA((len(masks),))],
        input_output_aliases={} if first else {len(masks): 0},
        compiler_params=pltpu.CompilerParams(vmem_limit_bytes=VMEM),
    )(*operands)


def shift(block, axis, size, step):
    return lax.ppermute(block, axis, [(i, (i + step) % size) for i in range(size)])


def ring(block, axis, size):
    return [block] + [shift(block, axis, size, step) for step in range(1, size)]


def pass_on(own, first, back, axis):
    me = lax.axis_index(axis)
    chosen = jnp.where(me == 2, first, jnp.where(me == 1, back, own))
    return lax.ppermute(chosen, axis, [(0, 2), (2, 3), (3, 1), (1, 0)])


def repeat_kernel(*refs):
    blocks, out = refs[:-2], refs[-1]
    at = 0
    for block in blocks:
        out[0, at : at + block.shape[0]] = block[...]
        at += block.shape[0]


def repeat(blocks, after, count):
    rows, width = sum(block.shape[0] for block in blocks), blocks[0].shape[1]
    return pl.pallas_call(
        repeat_kernel,
        grid=(count,),
        in_specs=[pl.BlockSpec(block.shape, lambda i: (0, 0)) for block in blocks] + [pl.BlockSpec(memory_space=pl.ANY)],
        out_specs=pl.BlockSpec((1, rows, width), lambda i: (i, 0, 0)),
        out_shape=jax.ShapeDtypeStruct((count, rows, width), blocks[0].dtype),
        compiler_params=pltpu.CompilerParams(vmem_limit_bytes=VMEM),
        cost_estimate=LONG,
    )(*blocks, after)


def local(cotangent, routes, gate_prob, hidden):
    n_section = lax.axis_size("section")
    n_expert = lax.axis_size("expert")
    section = lax.axis_index("section")
    expert = lax.axis_index("expert")
    mb_count = hidden.shape[2]
    tokens, width = cotangent.shape[1:]
    top = routes.shape[2]
    half_width = width // 2
    widths = [half_width * 5 // 8, half_width * 3 // 8]
    offsets = [sum(widths[:c]) for c in range(len(widths))]
    mirror = [(i, n_section - 1 - i) for i in range(n_section)]
    upper = section >= n_section // 2
    quarter = n_section // 4
    near, far = [], []
    for i in range(quarter // 2):
        near += [quarter + i, n_section - 1 - quarter - i, 2 * quarter + i, n_section - 1 - 2 * quarter - i]
    for i in range(quarter):
        far += [i, n_section - 1 - i]
    groups = [far, near]
    short = n_expert == 4
    cot = cotangent[0]
    given = lax.dynamic_slice_in_dim(cot, jnp.where(upper, 0, half_width), half_width, 1)
    kept = lax.dynamic_slice_in_dim(cot, jnp.where(upper, half_width, 0), half_width, 1)
    kept, routes, gate_prob = lax.optimization_barrier((kept, routes, gate_prob))
    kept = [kept[:, offset : offset + span] for offset, span in zip(offsets, widths)]
    meta = jnp.concatenate([routes[0].astype(jnp.float32), gate_prob[0]], 1).T.reshape(-1)
    metas = jnp.stack(ring(meta, "expert", n_expert)) if short else lax.all_gather(meta, "expert")
    acts = token_acts(metas, hidden[0, 0], groups, top, tokens // mb_count, short)
    taken = lax.ppermute(given, "section", mirror)
    taken = [taken[:, offset : offset + span] for offset, span in zip(offsets, widths)]
    if short:
        kept_first = shift(kept[0], "expert", n_expert, 1)
        *held, sent_back = lax.optimization_barrier((*acts, kept[0]))
        mirror_acts = [lax.ppermute(group, "section", mirror) for group in held]
        kept_back = shift(sent_back, "expert", n_expert, 3)
        kept_passed = pass_on(kept[0], kept_first, kept_back, "expert")
        taken_first, taken_back = shift(taken[0], "expert", n_expert, 1), shift(taken[0], "expert", n_expert, 3)
        taken_first, taken_back, mirror_acts[0] = lax.optimization_barrier((taken_first, taken_back, mirror_acts[0]))
        taken_passed = pass_on(taken[0], taken_first, taken_back, "expert")
        kept_passed, taken_passed, mirror_acts[1] = lax.optimization_barrier(
            (kept_passed, taken_passed, mirror_acts[1])
        )
        later = repeat([kept[1], taken[1]], taken_first, n_expert)
        later, taken_passed = lax.optimization_barrier((later, taken_passed))
        later = lax.all_to_all(later, "expert", split_axis=0, concat_axis=0, tiled=True)
        blocks = [kept[0], kept_first, kept_passed, kept_back, taken[0], taken_first, taken_passed, taken_back]
        cots = [[block[None] for block in blocks], [later]]
        layouts = [[(step, replica) for replica in range(2) for step in range(n_expert)], [(None, 0)]]
    else:
        mirror_acts = [lax.ppermute(group, "section", mirror) for group in acts]
        cots = [[lax.all_gather(jnp.concatenate([a, b]), "expert")] for a, b in zip(kept, taken)]
        layouts = [[(None, 0)]] * len(cots)

    out = None
    for c, (offset, span) in enumerate(zip(offsets, widths)):
        pieces = [None] * n_section
        for g, masks in enumerate(groups):
            parts = 2 if c == 0 else 1
            sums = []
            for part in range(parts):
                sums += product(acts[g], mirror_acts[g], cots[c], layouts[c], tokens, tile_of(span), part, parts)
            for mask, rows in zip(masks, sums):
                pieces[mask] = rows
                if mask:
                    pieces[mask] = lax.ppermute(rows, "section", [(i, i ^ mask) for i in range(n_section)])
        if c == 0:
            sent = [1, near[0], near[1], n_section - 2]
            early, cots[c + 1] = lax.optimization_barrier(([pieces[mask] for mask in sent], cots[c + 1]))
            for mask, rows in zip(sent, early):
                pieces[mask] = rows
        out = join(pieces, list(range(n_section)), n_section, offset, half_width, out)
    return out


def solution(mesh):
    return jax.shard_map(
        local,
        mesh=mesh,
        in_specs=(
            P("section", "expert", None),
            P("section", "expert", None),
            P("section", "expert", None),
            P("section", "expert", None, None, None),
        ),
        out_specs=P(None, "expert", "section", None),
        check_vma=False,
    )
```
